32 devices in a mesh: sweep: 4 (over y, x), azim: 8 (over z, core).
Axes of the slice: x: 2, y: 2, z: 4, core: 2. Of those that a mesh axis runs over, the one named last changes fastest.
Arguments:
- latents: bfloat16 [8, 8, 256, 512], P('sweep', None, 'azim'), may hold values from -6 to 6
- cotangent: bfloat16 [8, 8, 256, 512], P('sweep', None, 'azim'), may hold values from -6 to 6
- conv_kernel: float32 [9, 512], replicated, may hold values from -2 to 2
- conv_bias: float32 [512], replicated, may hold values from -3 to 3
- norm_gain: float32 [512], replicated, may hold values from 0.25 to 1.75
- w_query: bfloat16 [512, 256], replicated, may hold values from -2 to 2
- w_key: bfloat16 [512, 256], replicated, may hold values from -2 to 2
- w_value: bfloat16 [512, 256], replicated, may hold values from -0.25 to 0.25
- w_output: bfloat16 [512, 256], replicated, may hold values from -0.375 to 0.375
Outputs:
- grad_latents: float32 [8, 8, 256, 512], P('sweep', None, 'azim')
- grad_kernel: float32 [9, 512], replicated
- grad_bias: float32 [512], replicated
- grad_gain: float32 [512], replicated
- grad_query: float32 [512, 256], P('azim')
- grad_key: float32 [512, 256], P('azim')
- grad_value: float32 [512, 256], P('azim')
- grad_output: float32 [512, 256], P('azim')
The draws below stay inside these ranges and needn't reach their ends.
All inputs are finite; a program needn't handle non-finite values.
Results may differ from the reference program's by a relative error of at most 0.01.
The reference program's roundings to bfloat16 on the way count: a program that leaves them out, or rounds other values in their place, can miss the bound.
Values may be sent and summed in bfloat16 or wider, within the bound.
A program may use at most 64 MiB of HBM per device.

```python
import math
import jax
import jax.numpy as jnp
from jax import lax

C = 512
HEADS = 4
DH = 64
H = 8
SWEEPS = 8
W = 256
HD = 256
N_AZIM = 8


def projection_draw(key, salt):
    base = jax.random.normal(jax.random.fold_in(key, salt), (C, HEADS * DH), jnp.float32)
    base = jnp.clip(base, -4.0, 4.0) * C ** (-0.5)
    head_scale = jax.random.uniform(jax.random.fold_in(key, 7), (HEADS,), jnp.float32, 0.8, 1.25)
    columns = jnp.repeat(head_scale, DH)
    return jnp.clip(base * columns, -2.0, 2.0).astype(jnp.bfloat16)


def draw_w_query(key, part):
    return projection_draw(key, 11)


def draw_w_key(key, part):
    return projection_draw(key, 13)


def with_spikes(values, key, source, target, parts, factor):
    def block_of(dim):
        return (jnp.arange(values.shape[dim]) // (values.shape[dim] // parts)).reshape((-1,) + (1,) * (values.ndim - 1 - dim))

    one_side = jax.random.permutation(key, parts)[block_of(target)]
    second = (block_of(target) + parts // 2) % parts
    return jnp.where((block_of(source) == one_side) | (block_of(source) == second), factor * values, values)


def block_levels(stream_key, dims, split, least, largest):
    gain = 1.0
    for axis_at, parts in split:
        heights = jax.random.uniform(jax.random.fold_in(jax.random.fold_in(stream_key, 6), axis_at), (parts,), jnp.float32, least / len(split), largest / len(split))
        gain = gain * jnp.repeat(jnp.exp(heights), dims[axis_at] // parts).reshape((-1,) + (1,) * (len(dims) - 1 - axis_at))
    return gain


def gaussian(own_key, dims, spread, reach, pieces=(), kind=jnp.bfloat16):
    level = block_levels(own_key, dims, pieces, -0.22, 0.18) if pieces else 1.0
    entries = jax.random.normal(own_key, dims, jnp.float32) * spread * level
    return jnp.minimum(jnp.maximum(entries, -reach), reach).astype(kind)


def heavy_noise(rng, extent, scale, reach, shards, heavy, kind=jnp.bfloat16):
    values = scale * jax.random.normal(rng, extent, jnp.float32)
    if shards:
        values = values * block_levels(rng, extent, shards, -0.22, 0.18)
    return jnp.clip(with_spikes(values, jax.random.fold_in(rng, 3), *heavy), -reach, reach).astype(kind)


def setup_inputs(seed: int = 0) -> dict:
    key_list = jax.random.split(jax.random.key(seed), 10)
    return {
        "latents": gaussian(key_list[0], (SWEEPS, H, W, C), 1.0, 6.0, ((0, 4), (2, 8))),
        "cotangent": heavy_noise(key_list[1], (SWEEPS, H, W, C), 1.0, 6.0, ((0, 4), (2, 8)), (2, 3, 8, 2.0)),
        "conv_kernel": gaussian(key_list[2], (9, C), 0.35, 2.0, (), jnp.float32),
        "conv_bias": gaussian(key_list[3], (C,), 0.5, 3.0, (), jnp.float32),
        "norm_gain": jnp.clip(1.0 + 0.15 * jax.random.normal(key_list[4], (C,), jnp.float32), 0.25, 1.75),
        "w_query": draw_w_query(jax.random.fold_in(key_list[9], 71), 0),
        "w_key": draw_w_key(jax.random.fold_in(key_list[9], 71), 0),
        "w_value": gaussian(key_list[7], (C, HD), C ** -0.5, 0.25),
        "w_output": gaussian(key_list[8], (C, HD), HD ** -0.5, 0.375),
    }


EPS = 1e-06

def silu_slope(value):
    sigmoid_val = jax.nn.sigmoid(value)
    return sigmoid_val * (1.0 + value * (1.0 - sigmoid_val))

def frame_sweep(field):
    padded = jnp.pad(field, ((1, 1), (0, 0), (0, 0)))
    return jnp.concatenate([padded[:, -1:], padded, padded[:, :1]], axis=1)

def forward_sweep(latent_one, conv_kernel, conv_bias):
    height, width = (latent_one.shape[0], latent_one.shape[1])
    framed = frame_sweep(jax.nn.silu(latent_one.astype(jnp.float32)))
    conv_sum = jnp.zeros(latent_one.shape, jnp.float32)
    for row_tap in range(3):
        for col_tap in range(3):
            conv_sum = conv_sum + conv_kernel[3 * row_tap + col_tap] * framed[row_tap:row_tap + height, col_tap:col_tap + width]
    return (latent_one.astype(jnp.float32) + conv_sum + conv_bias).astype(jnp.bfloat16)

def attend(y_block, cot_block, w_query, w_key, w_value, w_output, norm_gain):
    sweeps, pixels, channels = y_block.shape
    heads = w_query.shape[1] // DH
    scale = 1.0 / math.sqrt(DH)
    y_float = y_block.astype(jnp.float32)
    root = jnp.sqrt(lax.optimization_barrier(jnp.mean(y_float * y_float, axis=-1, keepdims=True)) + EPS)
    inverse = 1.0 / root
    normed = (y_float * inverse * norm_gain).astype(jnp.bfloat16)
    rows = normed.reshape(sweeps * pixels, channels)
    query = jnp.dot(rows, w_query, preferred_element_type=jnp.float32).astype(jnp.bfloat16)
    key = jnp.dot(rows, w_key, preferred_element_type=jnp.float32).astype(jnp.bfloat16)
    value = jnp.dot(rows, w_value, preferred_element_type=jnp.float32).astype(jnp.bfloat16)
    query4 = query.reshape(sweeps, pixels, heads, DH).astype(jnp.float32)
    key4 = key.reshape(sweeps, pixels, heads, DH).astype(jnp.float32)
    value4 = value.reshape(sweeps, pixels, heads, DH).astype(jnp.float32)
    scores = jnp.einsum('tphd,uphd->phtu', query4, key4) * scale
    row_max = lax.optimization_barrier(jnp.max(scores, axis=-1, keepdims=True))
    expon = jnp.exp(scores - row_max)
    probs = expon / lax.optimization_barrier(jnp.sum(expon, axis=-1, keepdims=True))
    probs_low = probs.astype(jnp.bfloat16)
    attended = jnp.einsum('phtu,uphd->tphd', probs_low.astype(jnp.float32), value4).astype(jnp.bfloat16)
    attended_rows = attended.reshape(sweeps * pixels, heads * DH)
    cot_rows = cot_block.reshape(sweeps * pixels, channels)
    grad_output = jnp.dot(cot_rows.T, attended_rows, preferred_element_type=jnp.float32)
    grad_attended = jnp.dot(cot_rows, w_output, preferred_element_type=jnp.float32).astype(jnp.bfloat16)
    grad_att4 = grad_attended.reshape(sweeps, pixels, heads, DH).astype(jnp.float32)
    grad_probs = jnp.einsum('tphd,uphd->phtu', grad_att4, value4)
    grad_scores = (probs * (grad_probs - lax.optimization_barrier(jnp.sum(probs * grad_probs, axis=-1, keepdims=True))) * scale).astype(jnp.bfloat16)
    grad_v = jnp.einsum('phtu,tphd->uphd', probs_low.astype(jnp.float32), grad_att4).astype(jnp.bfloat16)
    grad_q = jnp.einsum('phtu,uphd->tphd', grad_scores.astype(jnp.float32), key4).astype(jnp.bfloat16)
    grad_k = jnp.einsum('phtu,tphd->uphd', grad_scores.astype(jnp.float32), query4).astype(jnp.bfloat16)
    grad_q = grad_q.reshape(sweeps * pixels, heads * DH)
    grad_k = grad_k.reshape(sweeps * pixels, heads * DH)
    grad_v = grad_v.reshape(sweeps * pixels, heads * DH)
    grad_query = jnp.dot(rows.T, grad_q, preferred_element_type=jnp.float32)
    grad_key = jnp.dot(rows.T, grad_k, preferred_element_type=jnp.float32)
    grad_value = jnp.dot(rows.T, grad_v, preferred_element_type=jnp.float32)
    grad_normed = jnp.dot(jnp.concatenate([grad_q, grad_k, grad_v], axis=-1), jnp.concatenate([w_query, w_key, w_value], axis=-1).T, preferred_element_type=jnp.float32)
    grad_normed = grad_normed.reshape(sweeps, pixels, channels)
    grad_gain = lax.optimization_barrier(jnp.sum(grad_normed * y_float * inverse, axis=(0, 1)))
    gained = grad_normed * norm_gain
    grad_attn = (inverse * (gained - y_float * lax.optimization_barrier(jnp.mean(gained * y_float, axis=-1, keepdims=True)) * inverse * inverse)).astype(jnp.bfloat16)
    return (grad_attn, grad_query, grad_key, grad_value, grad_output, grad_gain)

def reference(latents, cotangent, conv_kernel, conv_bias, norm_gain, w_query, w_key, w_value, w_output):
    sweeps, height, width, channels = latents.shape
    inner = w_query.shape[1]
    y_all = lax.map(lambda one: forward_sweep(one, conv_kernel, conv_bias), latents)
    blocks = N_AZIM
    block_pixels = height * width // blocks
    y_blocks = y_all.reshape(sweeps, blocks, block_pixels, channels).transpose(1, 0, 2, 3)
    cot_blocks = cotangent.reshape(sweeps, blocks, block_pixels, channels).transpose(1, 0, 2, 3)

    def step(carry, item):
        result = attend(item[0], item[1], w_query, w_key, w_value, w_output, norm_gain)
        carry = tuple((carry[idx] + result[idx + 1] for idx in range(5)))
        return (carry, result[0])
    zero_mat = jnp.zeros((channels, inner), jnp.float32)
    init = (zero_mat, zero_mat, zero_mat, zero_mat, jnp.zeros((channels,), jnp.float32))
    sums, grad_attn = lax.scan(step, init, (y_blocks, cot_blocks))
    grad_attn = grad_attn.transpose(1, 0, 2, 3).reshape(sweeps, height, width, channels)

    def backward_sweep(item):
        latent_one, cot_one, attn_one = item
        grad_y = cot_one.astype(jnp.float32) + attn_one.astype(jnp.float32)
        framed_act = frame_sweep(jax.nn.silu(latent_one.astype(jnp.float32)))
        framed_grad = frame_sweep(grad_y)
        grad_act = jnp.zeros(grad_y.shape, jnp.float32)
        taps = []
        for row_tap in range(3):
            for col_tap in range(3):
                weight = conv_kernel[3 * row_tap + col_tap]
                grad_act = grad_act + weight * framed_grad[2 - row_tap:2 - row_tap + height, 2 - col_tap:2 - col_tap + width]
                taps.append(lax.optimization_barrier(jnp.sum(grad_y * framed_act[row_tap:row_tap + height, col_tap:col_tap + width], axis=(0, 1))))
        latent_float = latent_one.astype(jnp.float32)
        grad_lat = grad_y + grad_act * silu_slope(latent_float)
        return (grad_lat, jnp.stack(taps), lax.optimization_barrier(jnp.sum(grad_y, axis=(0, 1))))
    grad_latents, tap_terms, bias_terms = lax.map(backward_sweep, (latents, cotangent, grad_attn))
    predivide = 1.0 / math.sqrt(sweeps * height * width)
    grad_kernel = lax.optimization_barrier(jnp.sum(tap_terms, axis=0)) * predivide
    grad_bias = lax.optimization_barrier(jnp.sum(bias_terms, axis=0)) * predivide
    return (grad_latents, grad_kernel, grad_bias, sums[4] * predivide, sums[0] * predivide, sums[1] * predivide, sums[2] * predivide, sums[3] * predivide)
```

```python
import functools
import math

import jax
import jax.numpy as jnp
from jax import lax
from jax.experimental import pallas as pl
from jax.experimental.pallas import tpu as pltpu
from jax.sharding import PartitionSpec as P

DH = 64
EPS = 1e-06
LANES = 128
PIX = 16
MESH = pl.DeviceIdType.MESH
VMEM = pl.BlockSpec(memory_space=pltpu.VMEM)
BIG = 56 * 1024 * 1024


def remote(src, dst, send, recv, where):
    return pltpu.make_async_remote_copy(
        src_ref=src, dst_ref=dst, send_sem=send, recv_sem=recv, device_id=where, device_id_type=MESH
    )


def greet(partners):
    barrier = pltpu.get_barrier_semaphore()
    for where in partners:
        pl.semaphore_signal(barrier, inc=1, device_id=where, device_id_type=MESH)
    pl.semaphore_wait(barrier, len(partners))


def store_shifted(dst, s, h, val):
    width = val.shape[0]
    dst[1, s, h + 1] = val
    dst[0, s, h + 1] = pltpu.roll(val, 1, 0)
    dst[2, s, h + 1] = pltpu.roll(val, width - 1, 0)


def patch_edges(dst, left, right, sweeps, height, width):
    for s in range(sweeps):
        for h in range(height):
            i = s * height + h
            dst[0, s, h + 1, 0:1, :] = left[i : i + 1, :]
            dst[2, s, h + 1, width - 1 : width, :] = right[i : i + 1, :]


def zero_frame(dst, sweeps, height):
    for b in range(3):
        for s in range(sweeps):
            dst[b, s, 0] = jnp.zeros(dst.shape[3:], jnp.float32)
            dst[b, s, height + 1] = jnp.zeros(dst.shape[3:], jnp.float32)


def forward_kernel(
    groups, strips, lat, cot, kern, bias, y_pix, cot_pix, halo_left, halo_right,
    act, y_src, edge_left, edge_right, a2a_send, a2a_recv, own_sem, halo_send, halo_recv,
):
    sweeps, height, width, channels = lat.shape
    each = height * width // groups
    me = lax.axis_index("sweep")
    az = lax.axis_index("azim")
    right, left = lax.rem(az + 1, strips), lax.rem(az + strips - 1, strips)
    partners = [lax.rem(me + k, groups) for k in range(1, groups)]
    greet([{"sweep": g} for g in partners] + [{"azim": left}, {"azim": right}])
    mine = pl.ds(pl.multiple_of(me * each, PIX), each)
    slots = pl.ds(me * sweeps, sweeps)

    def sends(src, out, at):
        copies = []
        for k, g in enumerate(partners):
            there = pl.ds(pl.multiple_of(g * each, PIX), each)
            copies.append(
                remote(src.at[:, there, :], out.at[slots], a2a_send.at[at, k], a2a_recv.at[at, k], {"sweep": g})
            )
        for copy in copies:
            copy.start()
        own = pltpu.make_async_copy(src.at[:, mine, :], out.at[slots], own_sem.at[at])
        own.start()
        return copies, own

    cot_copies, cot_own = sends(cot, cot_pix, 0)

    for s in range(sweeps):
        def activate(h, carry, s=s):
            x = lat[s, h].astype(jnp.float32)
            val = x / (1.0 + jnp.exp(-x))
            store_shifted(act, s, h, val)
            edge_left[pl.ds(s * height + h, 1), :] = val[0:1]
            edge_right[pl.ds(s * height + h, 1), :] = val[width - 1 : width]
            return carry
        lax.fori_loop(0, height, activate, 0)
    to_right = remote(edge_right, halo_left, halo_send.at[0], halo_recv.at[0], {"azim": right})
    to_left = remote(edge_left, halo_right, halo_send.at[1], halo_recv.at[1], {"azim": left})
    to_right.start()
    to_left.start()
    zero_frame(act, sweeps, height)
    to_right.wait()
    to_left.wait()
    patch_edges(act, halo_left, halo_right, sweeps, height, width)
    for s in range(sweeps):
        def convolve(h, carry, s=s):
            total = lat[s, h].astype(jnp.float32) + bias[...]
            for a in range(3):
                for b in range(3):
                    total = total + kern[3 * a + b : 3 * a + b + 1, :] * act[b, s, h + a]
            y_src[s, pl.ds(pl.multiple_of(h * width, PIX), width), :] = total.astype(jnp.bfloat16)
            return carry
        lax.fori_loop(0, height, convolve, 0)
    y_copies, y_own = sends(y_src, y_pix, 1)
    for copy in cot_copies + y_copies:
        copy.wait()
    cot_own.wait()
    y_own.wait()


def dot(a, b, dims):
    return lax.dot_general(a, b, (dims, ((), ())), preferred_element_type=jnp.float32)


NN = ((1,), (0,))
NT = ((1,), (1,))
TN = ((0,), (0,))


def attend_kernel(
    heads, y_ref, cot_ref, gain_ref, wq_ref, wk_ref, wv_ref, wo_ref, grad_ref, mats_ref, gain_out,
    rows_s, cot_s, att_s, gq_s, gk_s, gv_s,
):
    sweeps, pixels, channels = y_ref.shape
    inner = wq_ref.shape[1]
    m = sweeps * PIX
    scale = 1.0 / math.sqrt(DH)
    gain = gain_ref[...]
    wq, wk, wv, wo = wq_ref[...], wk_ref[...], wv_ref[...], wo_ref[...]
    row_pix = lax.broadcasted_iota(jnp.int32, (m, m), 0) % PIX
    col_pix = lax.broadcasted_iota(jnp.int32, (m, m), 1) % PIX
    same = row_pix == col_pix
    same = jnp.concatenate([same] * heads, axis=0)
    lane_head = lax.broadcasted_iota(jnp.int32, (1, inner), 1) // DH

    def spread(value):
        return jnp.concatenate(
            [jnp.where(lane_head == h, value, jnp.zeros_like(value)) for h in range(heads)], axis=0
        )

    def collect(value):
        total = jnp.where(lane_head == 0, value[0:m], 0.0)
        for h in range(1, heads):
            total = jnp.where(lane_head == h, value[h * m : (h + 1) * m], total)
        return total

    gain_total = jnp.zeros((1, channels), jnp.float32)
    for block in range(pixels // PIX):
        at = slice(block * PIX, (block + 1) * PIX)
        own = slice(block * m, (block + 1) * m)
        y = y_ref[:, at, :].reshape(m, channels).astype(jnp.float32)
        cot = cot_ref[:, at, :].reshape(m, channels)
        root = jnp.sqrt(jnp.mean(y * y, axis=-1, keepdims=True) + EPS)
        inverse = 1.0 / root
        normed = (y * inverse * gain).astype(jnp.bfloat16)
        rows_s[own, :] = normed
        cot_s[own, :] = cot
        query = dot(normed, wq, NN).astype(jnp.bfloat16)
        key = dot(normed, wk, NN).astype(jnp.bfloat16)
        value = dot(normed, wv, NN).astype(jnp.bfloat16)
        grad_att = dot(cot, wo, NN).astype(jnp.bfloat16)
        query_x = spread(query)
        grad_att_x = spread(grad_att)
        scores = jnp.where(same, dot(query_x, key, NT) * scale, -1e30)
        top = jnp.max(scores, axis=-1, keepdims=True)
        expon = jnp.exp(scores - top)
        probs = expon / jnp.sum(expon, axis=-1, keepdims=True)
        probs_low = probs.astype(jnp.bfloat16)
        att_s[own, :] = collect(dot(probs_low, value, NN)).astype(jnp.bfloat16)
        grad_probs = dot(grad_att_x, value, NT)
        inner_sum = jnp.sum(probs * grad_probs, axis=-1, keepdims=True)
        grad_scores = (probs * (grad_probs - inner_sum) * scale).astype(jnp.bfloat16)
        grad_v = dot(probs_low, grad_att_x, TN).astype(jnp.bfloat16)
        grad_q = collect(dot(grad_scores, key, NN)).astype(jnp.bfloat16)
        grad_k = dot(grad_scores, query_x, TN).astype(jnp.bfloat16)
        gq_s[own, :] = grad_q
        gk_s[own, :] = grad_k
        gv_s[own, :] = grad_v
        grad_normed = dot(grad_q, wq, NT) + dot(grad_k, wk, NT) + dot(grad_v, wv, NT)
        gain_total = gain_total + jnp.sum(grad_normed * y * inverse, axis=0, keepdims=True)
        gained = grad_normed * gain
        mean = jnp.mean(gained * y, axis=-1, keepdims=True)
        grad = inverse * (gained - y * mean * inverse * inverse)
        grad_ref[:, at, :] = grad.astype(jnp.bfloat16).reshape(sweeps, PIX, channels)
    gain_out[...] = gain_total
    per = inner // LANES
    for i, (left, right) in enumerate(
        ((rows_s, gq_s), (rows_s, gk_s), (rows_s, gv_s), (cot_s, att_s))
    ):
        full = dot(left[...], right[...], TN)
        for j in range(per):
            mats_ref[i * per + j] = full[:, j * LANES : (j + 1) * LANES]


def backward_kernel(
    groups, strips, predivide, grad, mats, cot, lat, kern, halo_left, halo_right, gain,
    out_lat, out_small, out_q, out_k, out_v, out_o,
    act, gy, ret, edge_left, edge_right, in_left, in_right, taps,
    pair_buf, acc, sweep_buf, acc2, z_buf, fin,
    small, small_pair, small_sweep, small_z,
    a2a_send, a2a_recv, own_sem, halo_send, halo_recv, pair_send, pair_recv,
    sweep_send, sweep_recv, z_send, z_recv, fin_send, fin_recv,
    sp_send, sp_recv, ss_send, ss_recv, sz_send, sz_recv,
):
    sweeps, height, width, channels = lat.shape
    each = height * width // groups
    planes = strips // 2
    me = lax.axis_index("sweep")
    az = lax.axis_index("azim")
    core = lax.rem(az, 2)
    z = az // 2
    other = az + 1 - 2 * core
    right, left = lax.rem(az + 1, strips), lax.rem(az + strips - 1, strips)
    partners = [lax.rem(me + k, groups) for k in range(1, groups)]
    z_partners = [lax.rem(z + k, planes) for k in range(1, planes)]
    greet(
        [{"sweep": g} for g in partners]
        + [{"azim": left}, {"azim": right}, {"azim": other}]
        + [{"azim": p * 2 + core} for p in z_partners]
    )
    mine = pl.ds(pl.multiple_of(me * each, PIX), each)
    slots = pl.ds(me * sweeps, sweeps)
    back = []
    for k, g in enumerate(partners):
        back.append(
            remote(grad.at[pl.ds(g * sweeps, sweeps)], ret.at[:, mine, :], a2a_send.at[k], a2a_recv.at[k], {"sweep": g})
        )
    for copy in back:
        copy.start()
    pair = remote(mats.at[:, :, 1 - core], pair_buf, pair_send, pair_recv, {"azim": other})
    pair.start()
    own = pltpu.make_async_copy(grad.at[slots], ret.at[:, mine, :], own_sem)
    own.start()

    for s in range(sweeps):
        def activate(h, carry, s=s):
            x = lat[s, h].astype(jnp.float32)
            store_shifted(act, s, h, x / (1.0 + jnp.exp(-x)))
            return carry
        lax.fori_loop(0, height, activate, 0)
    zero_frame(act, sweeps, height)
    zero_frame(gy, sweeps, height)
    patch_edges(act, halo_left, halo_right, sweeps, height, width)
    taps[...] = jnp.zeros(taps.shape, jnp.float32)

    for copy in back:
        copy.wait()
    own.wait()
    for s in range(sweeps):
        def combine(h, carry, s=s):
            got = ret[s, pl.ds(pl.multiple_of(h * width, PIX), width), :]
            val = cot[s, h].astype(jnp.float32) + got.astype(jnp.float32)
            store_shifted(gy, s, h, val)
            edge_left[pl.ds(s * height + h, 1), :] = val[0:1]
            edge_right[pl.ds(s * height + h, 1), :] = val[width - 1 : width]
            return carry
        lax.fori_loop(0, height, combine, 0)
    to_right = remote(edge_right, in_left, halo_send.at[0], halo_recv.at[0], {"azim": right})
    to_left = remote(edge_left, in_right, halo_send.at[1], halo_recv.at[1], {"azim": left})
    to_right.start()
    to_left.start()

    pair.wait()
    chunks, _, _, parts, rows, _ = mats.shape
    def add_pair(c, carry):
        for p in range(parts):
            for q in range(planes):
                acc[c * parts + p, q] = mats[c, q, core, p] + pair_buf[c, q, p]
        return carry
    lax.fori_loop(0, chunks, add_pair, 0)
    per = chunks * parts // groups
    scatter = []
    for k, g in enumerate(partners):
        scatter.append(
            remote(acc.at[pl.ds(g * per, per)], sweep_buf.at[k], sweep_send.at[k], sweep_recv.at[k], {"sweep": g})
        )
    for copy in scatter:
        copy.start()

    to_right.wait()
    to_left.wait()
    patch_edges(gy, in_left, in_right, sweeps, height, width)
    for s in range(sweeps):
        def convolve(h, carry, s=s):
            mid = gy[1, s, h + 1]
            total = jnp.zeros(mid.shape, jnp.float32)
            def fold(v):
                return sum(v[8 * i : 8 * i + 8] for i in range(1, width // 8)) + v[0:8]
            for a in range(3):
                for b in range(3):
                    t = 3 * a + b
                    total = total + kern[t : t + 1, :] * gy[2 - b, s, h + 2 - a]
                    taps[t] = taps[t] + fold(mid * act[b, s, h + a])
            taps[9] = taps[9] + fold(mid)
            x = lat[s, h].astype(jnp.float32)
            sig = 1.0 / (1.0 + jnp.exp(-x))
            out_lat[s, h] = mid + total * (sig * (1.0 + x * (1.0 - sig)))
            return carry
        lax.fori_loop(0, height, convolve, 0)
    small[...] = jnp.zeros(small.shape, jnp.float32)
    for t in range(10):
        small[t : t + 1, :] = jnp.sum(taps[t], axis=0, keepdims=True) * predivide
    small[10:11, :] = gain[...] * predivide
    sp = remote(small, small_pair, sp_send, sp_recv, {"azim": other})
    sp.start()

    for copy in scatter:
        copy.wait()
    for i in range(per):
        def add_sweep(q, carry, i=i):
            total = acc[me * per + i, q]
            for k in range(groups - 1):
                total = total + sweep_buf[k, i, q]
            acc2[q, i] = total
            return carry
        lax.fori_loop(0, planes, add_sweep, 0)
    along = []
    for k, p in enumerate(z_partners):
        along.append(
            remote(acc2.at[p], z_buf.at[k], z_send.at[k], z_recv.at[k], {"azim": p * 2 + core})
        )
    for copy in along:
        copy.start()

    sp.wait()
    small_sweep[me] = small[...] + small_pair[...]
    ss = []
    for k, g in enumerate(partners):
        ss.append(
            remote(small_sweep.at[me], small_sweep.at[me], ss_send.at[k], ss_recv.at[k], {"sweep": g})
        )
    for copy in ss:
        copy.start()

    for copy in along:
        copy.wait()
    for i in range(per):
        total = acc2[z, i]
        for k in range(planes - 1):
            total = total + z_buf[k, i]
        fin[me, i] = total * predivide
    gather = []
    for k, g in enumerate(partners):
        gather.append(
            remote(fin.at[me], fin.at[me], fin_send.at[k], fin_recv.at[k], {"sweep": g})
        )
    for copy in gather:
        copy.start()
    for copy in ss:
        copy.wait()
    total = small_sweep[0]
    for g in range(1, groups):
        total = total + small_sweep[g]
    small_z[z] = total
    sz = []
    for k, p in enumerate(z_partners):
        sz.append(
            remote(small_z.at[z], small_z.at[z], sz_send.at[k], sz_recv.at[k], {"azim": p * 2 + core})
        )
    for copy in sz:
        copy.start()
    for copy in gather:
        copy.wait()
    lanes = chunks // 4
    for g in range(groups):
        for i in range(per):
            c, p = divmod(g * per + i, parts)
            out = (out_q, out_k, out_v, out_o)[c // lanes]
            j = c % lanes
            out[p * rows : (p + 1) * rows, j * LANES : (j + 1) * LANES] = fin[g, i]
    for copy in sz:
        copy.wait()
    total = small_z[0]
    for p in range(1, planes):
        total = total + small_z[p]
    out_small[...] = total


def on_device(
    latents, cotangent, conv_kernel, conv_bias, norm_gain, w_query, w_key, w_value, w_output
):
    f32, bf16 = jnp.float32, jnp.bfloat16
    dma = pltpu.SemaphoreType.DMA
    sds = jax.ShapeDtypeStruct
    sweeps, height, width, channels = latents.shape
    inner = w_query.shape[1]
    groups = lax.axis_size("sweep")
    strips = lax.axis_size("azim")
    planes = strips // 2
    each = height * width // groups
    total = sweeps * groups
    tokens = total * each
    lines = sweeps * height
    edge = pltpu.VMEM((lines, channels), f32)
    framed = pltpu.VMEM((3, sweeps, height + 2, width, channels), f32)
    flat = (sweeps, height * width, channels)

    y_pix, cot_pix, halo_left, halo_right = pl.pallas_call(
        functools.partial(forward_kernel, groups, strips),
        out_shape=[
            sds((total, each, channels), bf16),
            sds((total, each, channels), bf16),
            sds((lines, channels), f32),
            sds((lines, channels), f32),
        ],
        in_specs=[VMEM] * 4,
        out_specs=[VMEM] * 4,
        scratch_shapes=[
            framed, pltpu.VMEM(flat, bf16), edge, edge,
            dma((2, groups - 1)), dma((2, groups - 1)), dma((2,)), dma((2,)), dma((2,)),
        ],
        compiler_params=pltpu.CompilerParams(
            collective_id=0, has_side_effects=True, vmem_limit_bytes=BIG
        ),
        name="conv_forward",
    )(latents, cotangent.reshape(flat), conv_kernel, conv_bias.reshape(1, channels))

    chunks = 4 * inner // LANES
    grad_attn, mats, gain = pl.pallas_call(
        functools.partial(attend_kernel, inner // DH),
        out_shape=[
            sds((total, each, channels), bf16),
            sds((chunks, channels, LANES), f32),
            sds((1, channels), f32),
        ],
        in_specs=[VMEM] * 7,
        out_specs=[VMEM] * 3,
        scratch_shapes=[
            pltpu.VMEM((tokens, channels), bf16),
            pltpu.VMEM((tokens, channels), bf16),
            pltpu.VMEM((tokens, inner), bf16),
            pltpu.VMEM((tokens, inner), bf16),
            pltpu.VMEM((tokens, inner), bf16),
            pltpu.VMEM((tokens, inner), bf16),
        ],
        compiler_params=pltpu.CompilerParams(vmem_limit_bytes=BIG),
        name="attend",
    )(y_pix, cot_pix, norm_gain.reshape(1, channels), w_query, w_key, w_value, w_output)

    rows_each = channels // strips
    parts = max(1, groups // chunks)
    rows = rows_each // parts
    per = chunks * parts // groups
    predivide = 1.0 / math.sqrt(total * height * width * strips)
    small_shape = (16, channels)
    out_mat = sds((rows_each, inner), f32)
    grad_latents, small, gq, gk, gv, go = pl.pallas_call(
        functools.partial(backward_kernel, groups, strips, predivide),
        out_shape=[
            sds(latents.shape, f32), sds(small_shape, f32), out_mat, out_mat, out_mat, out_mat,
        ],
        in_specs=[VMEM] * 8,
        out_specs=[VMEM] * 6,
        scratch_shapes=[
            framed, framed, pltpu.VMEM(flat, bf16), edge, edge, edge, edge,
            pltpu.VMEM((10, 8, channels), f32),
            pltpu.VMEM((chunks, planes, parts, rows, LANES), f32),
            pltpu.VMEM((chunks * parts, planes, rows, LANES), f32),
            pltpu.VMEM((groups - 1, per, planes, rows, LANES), f32),
            pltpu.VMEM((planes, per, rows, LANES), f32),
            pltpu.VMEM((planes - 1, per, rows, LANES), f32),
            pltpu.VMEM((groups, per, rows, LANES), f32),
            pltpu.VMEM(small_shape, f32),
            pltpu.VMEM(small_shape, f32),
            pltpu.VMEM((groups,) + small_shape, f32),
            pltpu.VMEM((planes,) + small_shape, f32),
            dma((groups - 1,)), dma((groups - 1,)), dma(()), dma((2,)), dma((2,)), dma(()), dma(()),
            dma((groups - 1,)), dma((groups - 1,)), dma((planes - 1,)), dma((planes - 1,)),
            dma((groups - 1,)), dma((groups - 1,)),
            dma(()), dma(()), dma((groups - 1,)), dma((groups - 1,)),
            dma((planes - 1,)), dma((planes - 1,)),
        ],
        compiler_params=pltpu.CompilerParams(
            collective_id=1, has_side_effects=True, vmem_limit_bytes=BIG
        ),
        name="conv_backward",
    )(
        grad_attn, mats.reshape(chunks, planes, 2, parts, rows, LANES), cotangent, latents,
        conv_kernel, halo_left, halo_right, gain,
    )
    return (grad_latents, small[:9], small[9], small[10], gq, gk, gv, go)


def solution(mesh):
    image = P("sweep", None, "azim", None)
    share = P("azim", None)
    return jax.shard_map(
        on_device,
        mesh=mesh,
        in_specs=(image, image) + (P(),) * 7,
        out_specs=(image, P(), P(), P(), share, share, share, share),
        check_vma=False,
    )
```

```python
import functools
import math

import jax
import jax.numpy as jnp
from jax import lax
from jax.experimental import pallas as pl
from jax.experimental.pallas import tpu as pltpu
from jax.sharding import PartitionSpec as P

DH = 64
EPS = 1e-06
LANES = 128
PIX = 16
MESH = pl.DeviceIdType.MESH
VMEM = pl.BlockSpec(memory_space=pltpu.VMEM)
ANY = pl.BlockSpec(memory_space=pl.ANY)
BIG = 56 * 1024 * 1024


def remote(src, dst, send, recv, where):
    return pltpu.make_async_remote_copy(
        src_ref=src, dst_ref=dst, send_sem=send, recv_sem=recv, device_id=where, device_id_type=MESH
    )


def greet(partners):
    barrier = pltpu.get_barrier_semaphore()
    for where in partners:
        pl.semaphore_signal(barrier, inc=1, device_id=where, device_id_type=MESH)
    pl.semaphore_wait(barrier, len(partners))


def store_shifted(dst, s, h, val):
    width = val.shape[0]
    dst[1, s, h + 1] = val
    dst[0, s, h + 1] = pltpu.roll(val, 1, 0)
    dst[2, s, h + 1] = pltpu.roll(val, width - 1, 0)


def patch_edges(dst, left, right, sweeps, height, width):
    for s in range(sweeps):
        for h in range(height):
            i = s * height + h
            dst[0, s, h + 1, 0:1, :] = left[i : i + 1, :]
            dst[2, s, h + 1, width - 1 : width, :] = right[i : i + 1, :]


def zero_frame(dst, sweeps, height):
    for b in range(3):
        for s in range(sweeps):
            dst[b, s, 0] = jnp.zeros(dst.shape[3:], jnp.float32)
            dst[b, s, height + 1] = jnp.zeros(dst.shape[3:], jnp.float32)


def dot(a, b, dims):
    return lax.dot_general(a, b, (dims, ((), ())), preferred_element_type=jnp.float32)


NN = ((1,), (0,))
NT = ((1,), (1,))
TN = ((0,), (0,))


def block_kernel(
    groups, strips, heads, predivide,
    lat, cot, cot_flat, kern, bias, gain_ref, wq_hbm, wk_hbm, wv_hbm, wo_hbm,
    out_lat, out_fin, out_small,
    act, gy, y_src, y_pix, cot_pix, grad, ret,
    fore_left, fore_right, fore_in_left, fore_in_right, edge_left, edge_right, in_left, in_right,
    weights, left_s, right_s, grad_att_s, mats, pair_buf, acc, sweep_buf, acc2, z_buf, lat_out,
    taps, small, small_pair, small_sweep, small_z,
    w_sem, own_sem, a2a_send, a2a_recv, back_send, back_recv, halo_send, halo_recv,
    pair_send, pair_recv, sweep_send, sweep_recv, z_send, z_recv, fin_send, fin_recv,
    sp_send, sp_recv, ss_send, ss_recv, sz_send, sz_recv, lat_sem,
):
    sweeps, height, width, channels = lat.shape
    each = height * width // groups
    planes = strips // 2
    inner = right_s.shape[2]
    me = lax.axis_index("sweep")
    az = lax.axis_index("azim")
    core = lax.rem(az, 2)
    z = az // 2
    other = az + 1 - 2 * core
    right, left = lax.rem(az + 1, strips), lax.rem(az + strips - 1, strips)
    partners = [lax.rem(me + k, groups) for k in range(1, groups)]
    z_partners = [lax.rem(z + k, planes) for k in range(1, planes)]
    pending = []

    def send(*args):
        copy = remote(*args)
        copy.start()
        pending.append(copy)
        return copy

    loads = []
    for i, w in enumerate((wq_hbm, wk_hbm, wv_hbm, wo_hbm)):
        loads.append(pltpu.make_async_copy(w, weights.at[i], w_sem.at[i]))
        loads[-1].start()
    greet(
        [{"sweep": g} for g in partners]
        + [{"azim": left}, {"azim": right}, {"azim": other}]
        + [{"azim": p * 2 + core} for p in z_partners]
    )
    mine = pl.ds(pl.multiple_of(me * each, PIX), each)
    slots = pl.ds(me * sweeps, sweeps)

    for s in range(sweeps):
        for h in range(height):
            i = s * height + h
            fore_left[i : i + 1, :] = lat[s, h, 0:16, :].astype(jnp.float32)[0:1]
            fore_right[i : i + 1, :] = lat[s, h, width - 16 : width, :].astype(jnp.float32)[15:16]
    to_right = send(fore_right, fore_in_left, halo_send.at[0], halo_recv.at[0], {"azim": right})
    to_left = send(fore_left, fore_in_right, halo_send.at[1], halo_recv.at[1], {"azim": left})

    def give(k, g, source, target, at):
        there = pl.ds(pl.multiple_of(g * each, PIX), each)
        return send(
            source.at[:, there, :], target.at[slots], a2a_send.at[at, k], a2a_recv.at[at, k], {"sweep": g}
        )

    cot_copies = [give(k, g, cot_flat, cot_pix, 0) for k, g in enumerate(partners)]
    cot_own = pltpu.make_async_copy(cot_flat.at[:, mine, :], cot_pix.at[slots], own_sem.at[0])
    cot_own.start()

    for s in range(sweeps):
        def activate(h, carry, s=s):
            x = lat[s, h].astype(jnp.float32)
            store_shifted(act, s, h, x / (1.0 + jnp.exp(-x)))
            return carry
        lax.fori_loop(0, height, activate, 0)
    zero_frame(act, sweeps, height)
    zero_frame(gy, sweeps, height)
    taps[...] = jnp.zeros(taps.shape, jnp.float32)
    to_right.wait_recv()
    to_left.wait_recv()
    for ref in (fore_in_left, fore_in_right):
        x = ref[...]
        ref[...] = x / (1.0 + jnp.exp(-x))
    patch_edges(act, fore_in_left, fore_in_right, sweeps, height, width)

    def convolve_row(s, h):
        total = lat[s, h].astype(jnp.float32) + bias[...]
        for a in range(3):
            for b in range(3):
                total = total + kern[3 * a + b : 3 * a + b + 1, :] * act[b, s, h + a]
        y_src[s, pl.ds(pl.multiple_of(h * width, PIX), width), :] = total.astype(jnp.bfloat16)

    y_copies = []
    lines = max(1, height // groups)
    if groups <= height:
        for k, g in enumerate(partners + [me]):
            def chunk(i, carry, g=g):
                convolve_row(i // lines, g * lines + i % lines)
                return carry
            lax.fori_loop(0, sweeps * lines, chunk, 0)
            if k < groups - 1:
                y_copies.append(give(k, g, y_src, y_pix, 1))
    else:
        def whole(i, carry):
            convolve_row(i // height, i % height)
            return carry
        lax.fori_loop(0, sweeps * height, whole, 0)
        y_copies = [give(k, g, y_src, y_pix, 1) for k, g in enumerate(partners)]
    y_own = pltpu.make_async_copy(y_src.at[:, mine, :], y_pix.at[slots], own_sem.at[1])
    y_own.start()

    m = groups * sweeps * PIX
    blocks = each // PIX
    total_sweeps = groups * sweeps
    scale = 1.0 / math.sqrt(DH)
    gain = gain_ref[...]
    for load in loads:
        load.wait()
    for copy in cot_copies:
        copy.wait_recv()
    cot_own.wait()
    for block in range(blocks):
        at = slice(block * PIX, (block + 1) * PIX)
        own = slice(block * m, (block + 1) * m)
        rows = cot_pix[:, at, :].reshape(m, channels)
        left_s[1, own, :] = rows
        grad_att_s[own, :] = dot(rows, weights[3], NN).astype(jnp.bfloat16)
    row_pix = lax.broadcasted_iota(jnp.int32, (m, m), 0) % PIX
    col_pix = lax.broadcasted_iota(jnp.int32, (m, m), 1) % PIX
    same = row_pix == col_pix
    same = jnp.concatenate([same] * heads, axis=0)
    lane_head = lax.broadcasted_iota(jnp.int32, (1, inner), 1) // DH

    def spread(value):
        return jnp.concatenate(
            [jnp.where(lane_head == h, value, jnp.zeros_like(value)) for h in range(heads)], axis=0
        )

    def collect(value):
        total = jnp.where(lane_head == 0, value[0:m], 0.0)
        for h in range(1, heads):
            total = jnp.where(lane_head == h, value[h * m : (h + 1) * m], total)
        return total

    for copy in y_copies:
        copy.wait_recv()
    y_own.wait()
    back, back_own = [], []
    gain_total = jnp.zeros((1, channels), jnp.float32)
    for block in range(blocks):
        at = slice(block * PIX, (block + 1) * PIX)
        own = slice(block * m, (block + 1) * m)
        y = y_pix[:, at, :].reshape(m, channels).astype(jnp.float32)
        root = jnp.sqrt(jnp.mean(y * y, axis=-1, keepdims=True) + EPS)
        inverse = 1.0 / root
        normed = (y * inverse * gain).astype(jnp.bfloat16)
        left_s[0, own, :] = normed
        query = dot(normed, weights[0], NN).astype(jnp.bfloat16)
        key = dot(normed, weights[1], NN).astype(jnp.bfloat16)
        value = dot(normed, weights[2], NN).astype(jnp.bfloat16)
        query_x = spread(query)
        grad_att_x = spread(grad_att_s[own, :])
        scores = jnp.where(same, dot(query_x, key, NT) * scale, -1e30)
        top = jnp.max(scores, axis=-1, keepdims=True)
        expon = jnp.exp(scores - top)
        probs = expon / jnp.sum(expon, axis=-1, keepdims=True)
        probs_low = probs.astype(jnp.bfloat16)
        right_s[3, own, :] = collect(dot(probs_low, value, NN)).astype(jnp.bfloat16)
        grad_probs = dot(grad_att_x, value, NT)
        inner_sum = jnp.sum(probs * grad_probs, axis=-1, keepdims=True)
        grad_scores = (probs * (grad_probs - inner_sum) * scale).astype(jnp.bfloat16)
        grad_v = dot(probs_low, grad_att_x, TN).astype(jnp.bfloat16)
        grad_q = collect(dot(grad_scores, key, NN)).astype(jnp.bfloat16)
        grad_k = dot(grad_scores, query_x, TN).astype(jnp.bfloat16)
        right_s[0, own, :] = grad_q
        right_s[1, own, :] = grad_k
        right_s[2, own, :] = grad_v
        grad_normed = (
            dot(grad_q, weights[0], NT) + dot(grad_k, weights[1], NT) + dot(grad_v, weights[2], NT)
        )
        gain_total = gain_total + jnp.sum(grad_normed * y * inverse, axis=0, keepdims=True)
        gained = grad_normed * gain
        mean = jnp.mean(gained * y, axis=-1, keepdims=True)
        grad_attn = inverse * (gained - y * mean * inverse * inverse)
        grad[:, at, :] = grad_attn.astype(jnp.bfloat16).reshape(total_sweeps, PIX, channels)
        here = pl.ds(pl.multiple_of(me * each + block * PIX, PIX), PIX)
        for k, g in enumerate(partners):
            back.append(
                send(
                    grad.at[pl.ds(g * sweeps, sweeps), at, :], ret.at[:, here, :],
                    back_send.at[block, k], back_recv.at[block, k], {"sweep": g},
                )
            )
        back_own.append(
            pltpu.make_async_copy(grad.at[slots, at, :], ret.at[:, here, :], own_sem.at[2 + block])
        )
        back_own[-1].start()

    _, lanes, _, _, parts, rows, _ = mats.shape
    per = 4 * lanes * parts // groups
    interleave = groups == 4
    order = [lax.rem(me + k + 1, 4) if interleave else k for k in range(4)]
    pairs = []
    for n, i in enumerate(order):
        full = dot(left_s[i // 3], right_s[i], TN)
        for j in range(lanes):
            part = full[:, j * LANES : (j + 1) * LANES]
            mats[i, j] = part.reshape(planes, 2, parts, rows, LANES)
        pairs.append(
            send(mats.at[i, :, :, 1 - core], pair_buf.at[i], pair_send.at[n], pair_recv.at[n], {"azim": other})
        )
    scatter = []

    def scatter_to(k, g):
        scatter.append(
            send(acc.at[pl.ds(g * per, per)], sweep_buf.at[k], sweep_send.at[k], sweep_recv.at[k], {"sweep": g})
        )

    for n, i in enumerate(order):
        pairs[n].wait_recv()
        for j in range(lanes):
            for p in range(parts):
                for q in range(planes):
                    acc[(i * lanes + j) * parts + p, q] = mats[i, j, q, core, p] + pair_buf[i, j, q, p]
        if interleave and n < 3:
            scatter_to(n, i)
    if not interleave:
        for k, g in enumerate(partners):
            scatter_to(k, g)

    for copy in back:
        copy.wait_recv()
    for copy in back_own:
        copy.wait()
    for s in range(sweeps):
        def combine(h, carry, s=s):
            got = ret[s, pl.ds(pl.multiple_of(h * width, PIX), width), :]
            val = cot[s, h].astype(jnp.float32) + got.astype(jnp.float32)
            store_shifted(gy, s, h, val)
            edge_left[pl.ds(s * height + h, 1), :] = val[0:1]
            edge_right[pl.ds(s * height + h, 1), :] = val[width - 1 : width]
            return carry
        lax.fori_loop(0, height, combine, 0)
    to_right = send(edge_right, in_left, halo_send.at[2], halo_recv.at[2], {"azim": right})
    to_left = send(edge_left, in_right, halo_send.at[3], halo_recv.at[3], {"azim": left})

    def fold(v):
        return sum(v[8 * i : 8 * i + 8] for i in range(1, width // 8)) + v[0:8]

    for s in range(sweeps):
        def weigh(h, carry, s=s):
            mid = gy[1, s, h + 1]
            for t in range(9):
                taps[t] = taps[t] + fold(mid * act[t % 3, s, h + t // 3])
            taps[9] = taps[9] + fold(mid)
            return carry
        lax.fori_loop(0, height, weigh, 0)
    small[...] = jnp.zeros(small.shape, jnp.float32)
    for t in range(10):
        small[t : t + 1, :] = jnp.sum(taps[t], axis=0, keepdims=True) * predivide
    small[10:11, :] = gain_total * predivide
    sp = send(small, small_pair, sp_send, sp_recv, {"azim": other})

    to_right.wait_recv()
    to_left.wait_recv()
    patch_edges(gy, in_left, in_right, sweeps, height, width)
    for s in range(sweeps):
        def convolve(h, carry, s=s):
            mid = gy[1, s, h + 1]
            total = jnp.zeros(mid.shape, jnp.float32)
            for a in range(3):
                for b in range(3):
                    t = 3 * a + b
                    total = total + kern[t : t + 1, :] * gy[2 - b, s, h + 2 - a]
            x = lat[s, h].astype(jnp.float32)
            sig = 1.0 / (1.0 + jnp.exp(-x))
            lat_out[s, h] = mid + total * (sig * (1.0 + x * (1.0 - sig)))
            return carry
        lax.fori_loop(0, height, convolve, 0)
    lat_copy = pltpu.make_async_copy(lat_out, out_lat, lat_sem)
    lat_copy.start()

    sp.wait_recv()
    small_sweep[me] = small[...] + small_pair[...]
    ss = []
    for k, g in enumerate(partners):
        ss.append(
            send(small_sweep.at[me], small_sweep.at[me], ss_send.at[k], ss_recv.at[k], {"sweep": g})
        )

    for copy in scatter:
        copy.wait_recv()
    along = []
    for k, p in enumerate(z_partners + [z]):
        for i in range(per):
            total = acc[me * per + i, p]
            for j in range(groups - 1):
                total = total + sweep_buf[j, i, p]
            acc2[p, i] = total
        if k < planes - 1:
            along.append(
                send(acc2.at[p], z_buf.at[k], z_send.at[k], z_recv.at[k], {"azim": p * 2 + core})
            )

    for copy in ss:
        copy.wait_recv()
    total = small_sweep[0]
    for g in range(1, groups):
        total = total + small_sweep[g]
    small_z[z] = total
    sz = []
    for k, p in enumerate(z_partners):
        sz.append(
            send(small_z.at[z], small_z.at[z], sz_send.at[k], sz_recv.at[k], {"azim": p * 2 + core})
        )

    for copy in along:
        copy.wait_recv()
    for i in range(per):
        total = acc2[z, i]
        for k in range(planes - 1):
            total = total + z_buf[k, i]
        out_fin[me, i] = total * predivide
    gather = []
    for k, g in enumerate(partners):
        gather.append(
            send(out_fin.at[me], out_fin.at[me], fin_send.at[k], fin_recv.at[k], {"sweep": g})
        )
    for copy in sz:
        copy.wait_recv()
    total = small_z[0]
    for p in range(1, planes):
        total = total + small_z[p]
    out_small[...] = total
    for copy in gather:
        copy.wait_recv()
    for copy in pending:
        copy.wait_send()
    lat_copy.wait()


def finish_kernel(parts, lat, fin, small, out_lat, out_kern, out_bias, out_gain, out_q, out_k, out_v, out_o, sems):
    copies = []
    for s in range(lat.shape[0]):
        for half in range(2):
            at = slice(half * lat.shape[1] // 2, (half + 1) * lat.shape[1] // 2)
            copies.append(pltpu.make_async_copy(lat.at[s, at], out_lat.at[s, at], sems.at[s, half]))
    for copy in copies:
        copy.start()
    groups, per, rows, _ = fin.shape
    lanes = groups * per // parts // 4
    for g in range(groups):
        for i in range(per):
            c, p = divmod(g * per + i, parts)
            out = (out_q, out_k, out_v, out_o)[c // lanes]
            j = c % lanes
            out[p * rows : (p + 1) * rows, j * LANES : (j + 1) * LANES] = fin[g, i]
    out_kern[...] = small[0:9, :]
    out_bias[...] = small[9:10, :]
    out_gain[...] = small[10:11, :]
    for copy in copies:
        copy.wait()


def on_device(
    latents, cotangent, conv_kernel, conv_bias, norm_gain, w_query, w_key, w_value, w_output
):
    f32, bf16 = jnp.float32, jnp.bfloat16
    dma = pltpu.SemaphoreType.DMA
    sds = jax.ShapeDtypeStruct
    sweeps, height, width, channels = latents.shape
    inner = w_query.shape[1]
    groups = lax.axis_size("sweep")
    strips = lax.axis_size("azim")
    planes = strips // 2
    each = height * width // groups
    total = sweeps * groups
    tokens = total * each
    edge = pltpu.VMEM((sweeps * height, channels), f32)
    framed = pltpu.VMEM((3, sweeps, height + 2, width, channels), f32)
    flat = (sweeps, height * width, channels)
    pixels = pltpu.VMEM((total, each, channels), bf16)
    lanes = inner // LANES
    chunks = 4 * lanes
    rows_each = channels // strips
    parts = max(1, groups // chunks)
    rows = rows_each // parts
    per = chunks * parts // groups
    predivide = 1.0 / math.sqrt(total * height * width * strips)
    small_shape = (16, channels)
    blocks = each // PIX
    to_sweep, to_z, one = dma((groups - 1,)), dma((planes - 1,)), dma(())

    raw_lat, fin, small = pl.pallas_call(
        functools.partial(block_kernel, groups, strips, inner // DH, predivide),
        out_shape=[
            sds(latents.shape, f32), sds((groups, per, rows, LANES), f32), sds(small_shape, f32),
        ],
        in_specs=[VMEM] * 6 + [ANY] * 4,
        out_specs=[ANY, VMEM, VMEM],
        scratch_shapes=[
            framed, framed, pltpu.VMEM(flat, bf16), pixels, pixels, pixels, pltpu.VMEM(flat, bf16),
            edge, edge, edge, edge, edge, edge, edge, edge,
            pltpu.VMEM((4, channels, inner), bf16),
            pltpu.VMEM((2, tokens, channels), bf16),
            pltpu.VMEM((4, tokens, inner), bf16),
            pltpu.VMEM((tokens, inner), bf16),
            pltpu.VMEM((4, lanes, planes, 2, parts, rows, LANES), f32),
            pltpu.VMEM((4, lanes, planes, parts, rows, LANES), f32),
            pltpu.VMEM((chunks * parts, planes, rows, LANES), f32),
            pltpu.VMEM((groups - 1, per, planes, rows, LANES), f32),
            pltpu.VMEM((planes, per, rows, LANES), f32),
            pltpu.VMEM((planes - 1, per, rows, LANES), f32),
            pltpu.VMEM(latents.shape, f32),
            pltpu.VMEM((10, 8, channels), f32),
            pltpu.VMEM(small_shape, f32),
            pltpu.VMEM(small_shape, f32),
            pltpu.VMEM((groups,) + small_shape, f32),
            pltpu.VMEM((planes,) + small_shape, f32),
            dma((4,)), dma((2 + blocks,)), dma((2, groups - 1)), dma((2, groups - 1)),
            dma((blocks, groups - 1)), dma((blocks, groups - 1)), dma((4,)), dma((4,)),
            dma((4,)), dma((4,)), to_sweep, to_sweep, to_z, to_z, to_sweep, to_sweep,
            one, one, to_sweep, to_sweep, to_z, to_z, one,
        ],
        compiler_params=pltpu.CompilerParams(
            collective_id=0, has_side_effects=True, vmem_limit_bytes=BIG
        ),
        name="block",
    )(
        latents, cotangent, cotangent.reshape(flat), conv_kernel, conv_bias.reshape(1, channels),
        norm_gain.reshape(1, channels), w_query, w_key, w_value, w_output,
    )
    out_mat, line = sds((rows_each, inner), f32), sds((1, channels), f32)
    out = pl.pallas_call(
        functools.partial(finish_kernel, parts),
        out_shape=[
            sds(latents.shape, f32), sds(conv_kernel.shape, f32), line, line,
            out_mat, out_mat, out_mat, out_mat,
        ],
        in_specs=[ANY, VMEM, VMEM],
        out_specs=[ANY] + [VMEM] * 7,
        scratch_shapes=[dma((sweeps, 2))],
        compiler_params=pltpu.CompilerParams(vmem_limit_bytes=BIG),
        name="finish",
    )(raw_lat, fin, small)
    grad_latents, grad_kernel, grad_bias, grad_gain, *mats = out
    return (grad_latents, grad_kernel, grad_bias.reshape(channels), grad_gain.reshape(channels), *mats)


def solution(mesh):
    image = P("sweep", None, "azim", None)
    share = P("azim", None)
    return jax.shard_map(
        on_device,
        mesh=mesh,
        in_specs=(image, image) + (P(),) * 7,
        out_specs=(image, P(), P(), P(), share, share, share, share),
        check_vma=False,
    )
```

```python
import functools
import math

import jax
import jax.numpy as jnp
from jax import lax
from jax.experimental import pallas as pl
from jax.experimental.pallas import tpu as pltpu
from jax.sharding import PartitionSpec as P

DH = 64
EPS = 1e-06
LANES = 128
PIX = 16
MESH = pl.DeviceIdType.MESH
VMEM = pl.BlockSpec(memory_space=pltpu.VMEM)
ANY = pl.BlockSpec(memory_space=pl.ANY)
BIG = 56 * 1024 * 1024


def remote(src, dst, send, recv, where):
    return pltpu.make_async_remote_copy(
        src_ref=src, dst_ref=dst, send_sem=send, recv_sem=recv, device_id=where, device_id_type=MESH
    )


def greet(partners):
    barrier = pltpu.get_barrier_semaphore()
    for where in partners:
        pl.semaphore_signal(barrier, inc=1, device_id=where, device_id_type=MESH)
    pl.semaphore_wait(barrier, len(partners))


def store_shifted(dst, s, h, val):
    width = val.shape[0]
    dst[1, s, h + 1] = val
    dst[0, s, h + 1] = pltpu.roll(val, 1, 0)
    dst[2, s, h + 1] = pltpu.roll(val, width - 1, 0)


def patch_edges(dst, left, right, sweeps, height, width):
    for s in range(sweeps):
        for h in range(height):
            i = s * height + h
            dst[0, s, h + 1, 0:1, :] = left[i : i + 1, :]
            dst[2, s, h + 1, width - 1 : width, :] = right[i : i + 1, :]


def zero_frame(dst, sweeps, height):
    for b in range(3):
        for s in range(sweeps):
            dst[b, s, 0] = jnp.zeros(dst.shape[3:], jnp.float32)
            dst[b, s, height + 1] = jnp.zeros(dst.shape[3:], jnp.float32)


def dot(a, b, dims):
    return lax.dot_general(a, b, (dims, ((), ())), preferred_element_type=jnp.float32)


NN = ((1,), (0,))
NT = ((1,), (1,))
TN = ((0,), (0,))


def block_kernel(
    groups, strips, heads, predivide,
    lat, cot, kern, bias, gain_ref, wq_hbm, wk_hbm, wv_hbm, wo_hbm,
    out_lat, out_fin, out_small,
    act, gy, y_src, y_pix, cot_pix, grad, ret,
    fore_left, fore_right, fore_in_left, fore_in_right, edge_left, edge_right, in_left, in_right,
    weights, left_s, right_s, grad_att_s, mats, pair_buf, acc, sweep_buf, acc2, z_buf, early_z, early_sum, late_buf, lat_out,
    taps, small, small_pair, small_sweep, small_z,
    w_sem, own_sem, a2a_send, a2a_recv, back_send, back_recv, halo_send, halo_recv,
    pair_send, pair_recv, sweep_send, sweep_recv, z_send, z_recv, fin_send, fin_recv,
    sp_send, sp_recv, ss_send, ss_recv, sz_send, sz_recv, lat_sem, ez_send, ez_recv, late_send, late_recv,
):
    sweeps, height, width, channels = lat.shape
    each = height * width // groups
    planes = strips // 2
    inner = right_s.shape[2]
    me = lax.axis_index("sweep")
    az = lax.axis_index("azim")
    core = lax.rem(az, 2)
    z = az // 2
    other = az + 1 - 2 * core
    right, left = lax.rem(az + 1, strips), lax.rem(az + strips - 1, strips)
    partners = [lax.rem(me + k, groups) for k in range(1, groups)]
    z_partners = [lax.rem(z + k, planes) for k in range(1, planes)]
    pending = []

    def send(*args):
        copy = remote(*args)
        copy.start()
        pending.append(copy)
        return copy

    loads = []
    for i, w in enumerate((wq_hbm, wk_hbm, wv_hbm, wo_hbm)):
        loads.append(pltpu.make_async_copy(w, weights.at[i], w_sem.at[i]))
        loads[-1].start()
    greet(
        [{"sweep": g} for g in partners]
        + [{"azim": left}, {"azim": right}, {"azim": other}]
        + [{"azim": p * 2 + core} for p in z_partners]
    )
    mine = pl.ds(pl.multiple_of(me * each, PIX), each)
    slots = pl.ds(me * sweeps, sweeps)

    for s in range(sweeps):
        for h in range(height):
            i = s * height + h
            fore_left[i : i + 1, :] = lat[s, h, 0:16, :].astype(jnp.float32)[0:1]
            fore_right[i : i + 1, :] = lat[s, h, width - 16 : width, :].astype(jnp.float32)[15:16]
    to_right = send(fore_right, fore_in_left, halo_send.at[0], halo_recv.at[0], {"azim": right})
    to_left = send(fore_left, fore_in_right, halo_send.at[1], halo_recv.at[1], {"azim": left})

    def give(k, g, source, target, stage, count, send_sem, recv_sem):
        there = pl.ds(pl.multiple_of(g * each + stage * count, PIX), count)
        here = slice(stage * count, (stage + 1) * count)
        return send(source.at[:, there, :], target.at[slots, here, :], send_sem, recv_sem, {"sweep": g})

    cot_copies = [give(k, g, cot, cot_pix, 0, each, a2a_send.at[0, k], a2a_recv.at[0, k]) for k, g in enumerate(partners)]
    cot_own = pltpu.make_async_copy(cot.at[:, mine, :], cot_pix.at[slots], own_sem.at[0])
    cot_own.start()

    for s in range(sweeps):
        def activate(h, carry, s=s):
            x = lat[s, h].astype(jnp.float32)
            store_shifted(act, s, h, x / (1.0 + jnp.exp(-x)))
            return carry
        lax.fori_loop(0, height, activate, 0)
    zero_frame(act, sweeps, height)
    zero_frame(gy, sweeps, height)
    taps[...] = jnp.zeros(taps.shape, jnp.float32)
    to_right.wait_recv()
    to_left.wait_recv()
    for ref in (fore_in_left, fore_in_right):
        x = ref[...]
        ref[...] = x / (1.0 + jnp.exp(-x))
    patch_edges(act, fore_in_left, fore_in_right, sweeps, height, width)

    def convolve_row(s, h):
        total = lat[s, h].astype(jnp.float32) + bias[...]
        for a in range(3):
            for b in range(3):
                total = total + kern[3 * a + b : 3 * a + b + 1, :] * act[b, s, h + a]
        y_src[s, pl.ds(pl.multiple_of(h * width, PIX), width), :] = total.astype(jnp.bfloat16)

    lines = height // groups if groups <= height else 1
    count = each // lines
    y_copies = [[] for _ in range(lines)]

    def give_y(k, g, stage):
        y_copies[stage].append(
            give(k, g, y_src, y_pix, stage, count, a2a_send.at[1 + stage, k], a2a_recv.at[1 + stage, k])
        )

    if groups <= height:
        for stage in range(lines):
            for k, g in enumerate(partners + [me]):
                for sweep in range(sweeps):
                    convolve_row(sweep, g * lines + stage)
                if k < groups - 1:
                    give_y(k, g, stage)
    else:
        def whole(i, carry):
            convolve_row(i // height, i % height)
            return carry
        lax.fori_loop(0, sweeps * height, whole, 0)
        for k, g in enumerate(partners):
            give_y(k, g, 0)
    y_own = pltpu.make_async_copy(y_src.at[:, mine, :], y_pix.at[slots], own_sem.at[1])
    y_own.start()

    m = groups * sweeps * PIX
    blocks = each // PIX
    total_sweeps = groups * sweeps
    scale = 1.0 / math.sqrt(DH)
    gain = gain_ref[...]
    for load in loads:
        load.wait()
    for copy in cot_copies:
        copy.wait_recv()
    cot_own.wait()
    for block in range(blocks):
        at = slice(block * PIX, (block + 1) * PIX)
        own = slice(block * m, (block + 1) * m)
        rows = cot_pix[:, at, :].reshape(m, channels)
        left_s[1, own, :] = rows
        grad_att_s[own, :] = dot(rows, weights[3], NN).astype(jnp.bfloat16)
    row_pix = lax.broadcasted_iota(jnp.int32, (m, m), 0) % PIX
    col_pix = lax.broadcasted_iota(jnp.int32, (m, m), 1) % PIX
    same = row_pix == col_pix
    same = jnp.concatenate([same] * heads, axis=0)
    lane_head = lax.broadcasted_iota(jnp.int32, (1, inner), 1) // DH

    def spread(value):
        return jnp.concatenate(
            [jnp.where(lane_head == h, value, jnp.zeros_like(value)) for h in range(heads)], axis=0
        )

    def collect(value):
        total = jnp.where(lane_head == 0, value[0:m], 0.0)
        for h in range(1, heads):
            total = jnp.where(lane_head == h, value[h * m : (h + 1) * m], total)
        return total

    y_own.wait()
    back, back_own = [], []
    gain_total = jnp.zeros((1, channels), jnp.float32)
    several = count // PIX
    for stage in range(lines):
        for copy in y_copies[stage]:
            copy.wait_recv()
        base = stage * count
        span = slice(stage * several * m, (stage + 1) * several * m)
        y = jnp.concatenate(
            [
                y_pix[:, base + i * PIX : base + (i + 1) * PIX, :].reshape(m, channels)
                for i in range(several)
            ],
            axis=0,
        ).astype(jnp.float32)
        root = jnp.sqrt(jnp.mean(y * y, axis=-1, keepdims=True) + EPS)
        inverse = 1.0 / root
        normed = (y * inverse * gain).astype(jnp.bfloat16)
        left_s[0, span, :] = normed
        queries = dot(normed, weights[0], NN).astype(jnp.bfloat16)
        keys = dot(normed, weights[1], NN).astype(jnp.bfloat16)
        values = dot(normed, weights[2], NN).astype(jnp.bfloat16)
        grads = []
        for i in range(several):
            part = slice(i * m, (i + 1) * m)
            own = slice((stage * several + i) * m, (stage * several + i + 1) * m)
            key, value = keys[part], values[part]
            query_x = spread(queries[part])
            grad_att_x = spread(grad_att_s[own, :])
            scores = jnp.where(same, dot(query_x, key, NT) * scale, -1e30)
            top = jnp.max(scores, axis=-1, keepdims=True)
            expon = jnp.exp(scores - top)
            probs = expon / jnp.sum(expon, axis=-1, keepdims=True)
            probs_low = probs.astype(jnp.bfloat16)
            right_s[3, own, :] = collect(dot(probs_low, value, NN)).astype(jnp.bfloat16)
            grad_probs = dot(grad_att_x, value, NT)
            inner_sum = jnp.sum(probs * grad_probs, axis=-1, keepdims=True)
            grad_scores = (probs * (grad_probs - inner_sum) * scale).astype(jnp.bfloat16)
            grad_v = dot(probs_low, grad_att_x, TN).astype(jnp.bfloat16)
            grad_q = collect(dot(grad_scores, key, NN)).astype(jnp.bfloat16)
            grad_k = dot(grad_scores, query_x, TN).astype(jnp.bfloat16)
            right_s[0, own, :] = grad_q
            right_s[1, own, :] = grad_k
            right_s[2, own, :] = grad_v
            grads.append((grad_q, grad_k, grad_v))
        grad_q, grad_k, grad_v = (jnp.concatenate(each_grad, axis=0) for each_grad in zip(*grads))
        grad_normed = (
            dot(grad_q, weights[0], NT) + dot(grad_k, weights[1], NT) + dot(grad_v, weights[2], NT)
        )
        gain_total = gain_total + jnp.sum(grad_normed * y * inverse, axis=0, keepdims=True)
        gained = grad_normed * gain
        mean = jnp.mean(gained * y, axis=-1, keepdims=True)
        grad_attn = (inverse * (gained - y * mean * inverse * inverse)).astype(jnp.bfloat16)
        for i in range(several):
            at = slice(base + i * PIX, base + (i + 1) * PIX)
            grad[:, at, :] = grad_attn[i * m : (i + 1) * m].reshape(total_sweeps, PIX, channels)
        at = slice(base, base + count)
        here = pl.ds(pl.multiple_of(me * each + base, PIX), count)
        for k, g in enumerate(partners):
            back.append(
                send(
                    grad.at[pl.ds(g * sweeps, sweeps), at, :], ret.at[:, here, :],
                    back_send.at[stage, k], back_recv.at[stage, k], {"sweep": g},
                )
            )
        back_own.append(
            pltpu.make_async_copy(grad.at[slots, at, :], ret.at[:, here, :], own_sem.at[2 + stage])
        )
        back_own[-1].start()

    _, lanes, _, _, parts, rows, _ = mats.shape
    per = 4 * lanes * parts // groups
    interleave = groups == 4
    order = [lax.rem(me + k + 1, 4) if interleave else k for k in range(4)]
    pairs = []
    for n, i in enumerate(order):
        full = dot(left_s[i // 3], right_s[i], TN)
        for j in range(lanes):
            part = full[:, j * LANES : (j + 1) * LANES]
            mats[i, j] = part.reshape(planes, 2, parts, rows, LANES)
        pairs.append(
            send(mats.at[i, :, :, 1 - core], pair_buf.at[i], pair_send.at[n], pair_recv.at[n], {"azim": other})
        )
    scatter, early = [], []
    units = lanes * parts
    split = rows - rows * 3 // 8 // 8 * 8

    def scatter_to(k, g):
        scatter.append(
            send(acc.at[pl.ds(g * per, per), :, 0:split], sweep_buf.at[k], sweep_send.at[k], sweep_recv.at[k], {"sweep": g})
        )

    for n, i in enumerate(order):
        pairs[n].wait_recv()
        for j in range(lanes):
            for p in range(parts):
                for q in range(planes):
                    acc[(i * lanes + j) * parts + p, q] = mats[i, j, q, core, p] + pair_buf[i, j, q, p]
        if interleave and n < 3:
            scatter_to(n, i)
        if split < rows:
            of = pl.ds(i * units, units)
            for k, p in enumerate(z_partners):
                early.append(
                    send(
                        acc.at[of, p, split:rows], early_z.at[k, of], ez_send.at[n, k], ez_recv.at[n, k],
                        {"azim": p * 2 + core},
                    )
                )
    if not interleave:
        for k, g in enumerate(partners):
            scatter_to(k, g)

    for copy in back:
        copy.wait_recv()
    for copy in back_own:
        copy.wait()
    for s in range(sweeps):
        def combine(h, carry, s=s):
            at = pl.ds(pl.multiple_of(h * width, PIX), width)
            val = cot[s, at, :].astype(jnp.float32) + ret[s, at, :].astype(jnp.float32)
            store_shifted(gy, s, h, val)
            edge_left[pl.ds(s * height + h, 1), :] = val[0:1]
            edge_right[pl.ds(s * height + h, 1), :] = val[width - 1 : width]
            return carry
        lax.fori_loop(0, height, combine, 0)
    to_right = send(edge_right, in_left, halo_send.at[2], halo_recv.at[2], {"azim": right})
    to_left = send(edge_left, in_right, halo_send.at[3], halo_recv.at[3], {"azim": left})

    def fold(v):
        return sum(v[8 * i : 8 * i + 8] for i in range(1, width // 8)) + v[0:8]

    for s in range(sweeps):
        def weigh(h, carry, s=s):
            mid = gy[1, s, h + 1]
            for t in range(9):
                taps[t] = taps[t] + fold(mid * act[t % 3, s, h + t // 3])
            taps[9] = taps[9] + fold(mid)
            return carry
        lax.fori_loop(0, height, weigh, 0)
    small[...] = jnp.zeros(small.shape, jnp.float32)
    for t in range(10):
        small[t : t + 1, :] = jnp.sum(taps[t], axis=0, keepdims=True) * predivide
    small[10:11, :] = gain_total * predivide
    sp = send(small, small_pair, sp_send, sp_recv, {"azim": other})

    to_right.wait_recv()
    to_left.wait_recv()
    patch_edges(gy, in_left, in_right, sweeps, height, width)
    for s in range(sweeps):
        def convolve(h, carry, s=s):
            mid = gy[1, s, h + 1]
            total = jnp.zeros(mid.shape, jnp.float32)
            for a in range(3):
                for b in range(3):
                    t = 3 * a + b
                    total = total + kern[t : t + 1, :] * gy[2 - b, s, h + 2 - a]
            x = lat[s, h].astype(jnp.float32)
            sig = 1.0 / (1.0 + jnp.exp(-x))
            lat_out[s, h] = mid + total * (sig * (1.0 + x * (1.0 - sig)))
            return carry
        lax.fori_loop(0, height, convolve, 0)
    lat_copy = pltpu.make_async_copy(lat_out, out_lat, lat_sem)
    lat_copy.start()

    sp.wait_recv()
    small_sweep[me] = small[...] + small_pair[...]
    ss = []
    for k, g in enumerate(partners):
        ss.append(
            send(small_sweep.at[me], small_sweep.at[me], ss_send.at[k], ss_recv.at[k], {"sweep": g})
        )

    late = []
    if split < rows:
        for copy in early:
            copy.wait_recv()
        for k, g in enumerate(partners + [me]):
            for i in range(per):
                u = g * per + i
                total = acc[u, z, split:rows]
                for j in range(planes - 1):
                    total = total + early_z[j, u]
                early_sum[u] = total
            if k < groups - 1:
                late.append(
                    send(
                        early_sum.at[pl.ds(g * per, per)], late_buf.at[k], late_send.at[k], late_recv.at[k],
                        {"sweep": g},
                    )
                )
    for copy in scatter:
        copy.wait_recv()
    along = []
    for k, p in enumerate(z_partners + [z]):
        for i in range(per):
            total = acc[me * per + i, p, 0:split]
            for j in range(groups - 1):
                total = total + sweep_buf[j, i, p]
            acc2[p, i] = total
        if k < planes - 1:
            along.append(
                send(acc2.at[p], z_buf.at[k], z_send.at[k], z_recv.at[k], {"azim": p * 2 + core})
            )

    for copy in ss:
        copy.wait_recv()
    total = small_sweep[0]
    for g in range(1, groups):
        total = total + small_sweep[g]
    small_z[z] = total
    sz = []
    for k, p in enumerate(z_partners):
        sz.append(
            send(small_z.at[z], small_z.at[z], sz_send.at[k], sz_recv.at[k], {"azim": p * 2 + core})
        )

    gather = []
    if split < rows:
        for copy in late:
            copy.wait_recv()
        for i in range(per):
            total = early_sum[me * per + i]
            for k in range(groups - 1):
                total = total + late_buf[k, i]
            out_fin[me, i, split:rows] = total * predivide
        for k, g in enumerate(partners):
            some = out_fin.at[me, :, split:rows]
            gather.append(send(some, some, fin_send.at[1, k], fin_recv.at[1, k], {"sweep": g}))
    for copy in along:
        copy.wait_recv()
    for i in range(per):
        total = acc2[z, i]
        for k in range(planes - 1):
            total = total + z_buf[k, i]
        out_fin[me, i, 0:split] = total * predivide
    for k, g in enumerate(partners):
        some = out_fin.at[me, :, 0:split]
        gather.append(send(some, some, fin_send.at[0, k], fin_recv.at[0, k], {"sweep": g}))
    for copy in sz:
        copy.wait_recv()
    total = small_z[0]
    for p in range(1, planes):
        total = total + small_z[p]
    out_small[...] = total
    for copy in gather:
        copy.wait_recv()
    for copy in pending:
        copy.wait_send()
    lat_copy.wait()


def finish_kernel(parts, lat, fin, small, out_lat, out_kern, out_bias, out_gain, out_q, out_k, out_v, out_o):
    out_lat[...] = lat[...]

    @pl.when(pl.program_id(0) == 0)
    def unpack():
        groups, per, rows, _ = fin.shape
        lanes = groups * per // parts // 4
        for g in range(groups):
            for i in range(per):
                c, p = divmod(g * per + i, parts)
                out = (out_q, out_k, out_v, out_o)[c // lanes]
                j = c % lanes
                out[p * rows : (p + 1) * rows, j * LANES : (j + 1) * LANES] = fin[g, i]
        out_kern[...] = small[0:9, :]
        out_bias[...] = small[9:10, :]
        out_gain[...] = small[10:11, :]


def whole_block(shape):
    return pl.BlockSpec(shape, lambda i: (0,) * len(shape))


def on_device(
    latents, cotangent, conv_kernel, conv_bias, norm_gain, w_query, w_key, w_value, w_output
):
    f32, bf16 = jnp.float32, jnp.bfloat16
    dma = pltpu.SemaphoreType.DMA
    sds = jax.ShapeDtypeStruct
    sweeps, height, width, channels = latents.shape
    inner = w_query.shape[1]
    groups = lax.axis_size("sweep")
    strips = lax.axis_size("azim")
    planes = strips // 2
    each = height * width // groups
    total = sweeps * groups
    tokens = total * each
    edge = pltpu.VMEM((sweeps * height, channels), f32)
    framed = pltpu.VMEM((3, sweeps, height + 2, width, channels), f32)
    flat = (sweeps, height * width, channels)
    pixels = pltpu.VMEM((total, each, channels), bf16)
    lanes = inner // LANES
    chunks = 4 * lanes
    rows_each = channels // strips
    parts = max(1, groups // chunks)
    rows = rows_each // parts
    per = chunks * parts // groups
    predivide = 1.0 / math.sqrt(total * height * width * strips)
    small_shape = (16, channels)
    lines = height // groups if groups <= height else 1
    second = rows * 3 // 8 // 8 * 8
    to_sweep, to_z, one = dma((groups - 1,)), dma((planes - 1,)), dma(())

    raw_lat, fin, small = pl.pallas_call(
        functools.partial(block_kernel, groups, strips, inner // DH, predivide),
        out_shape=[
            sds(latents.shape, f32), sds((groups, per, rows, LANES), f32), sds(small_shape, f32),
        ],
        in_specs=[VMEM] * 5 + [ANY] * 4,
        out_specs=[ANY, VMEM, VMEM],
        scratch_shapes=[
            framed, framed, pltpu.VMEM(flat, bf16), pixels, pixels, pixels, pltpu.VMEM(flat, bf16),
            edge, edge, edge, edge, edge, edge, edge, edge,
            pltpu.VMEM((4, channels, inner), bf16),
            pltpu.VMEM((2, tokens, channels), bf16),
            pltpu.VMEM((4, tokens, inner), bf16),
            pltpu.VMEM((tokens, inner), bf16),
            pltpu.VMEM((4, lanes, planes, 2, parts, rows, LANES), f32),
            pltpu.VMEM((4, lanes, planes, parts, rows, LANES), f32),
            pltpu.VMEM((chunks * parts, planes, rows, LANES), f32),
            pltpu.VMEM((groups - 1, per, planes, rows - second, LANES), f32),
            pltpu.VMEM((planes, per, rows - second, LANES), f32),
            pltpu.VMEM((planes - 1, per, rows - second, LANES), f32),
            pltpu.VMEM((planes - 1, chunks * parts, max(8, second), LANES), f32),
            pltpu.VMEM((chunks * parts, max(8, second), LANES), f32),
            pltpu.VMEM((groups - 1, per, max(8, second), LANES), f32),
            pltpu.VMEM(latents.shape, f32),
            pltpu.VMEM((10, 8, channels), f32),
            pltpu.VMEM(small_shape, f32),
            pltpu.VMEM(small_shape, f32),
            pltpu.VMEM((groups,) + small_shape, f32),
            pltpu.VMEM((planes,) + small_shape, f32),
            dma((4,)), dma((2 + lines,)), dma((1 + lines, groups - 1)), dma((1 + lines, groups - 1)),
            dma((lines, groups - 1)), dma((lines, groups - 1)), dma((4,)), dma((4,)),
            dma((4,)), dma((4,)), to_sweep, to_sweep, to_z, to_z, dma((2, groups - 1)), dma((2, groups - 1)),
            one, one, to_sweep, to_sweep, to_z, to_z, one,
            dma((4, planes - 1)), dma((4, planes - 1)), to_sweep, to_sweep,
        ],
        compiler_params=pltpu.CompilerParams(
            collective_id=0, has_side_effects=True, vmem_limit_bytes=BIG
        ),
        name="block",
    )(
        latents, cotangent.reshape(flat), conv_kernel, conv_bias.reshape(1, channels),
        norm_gain.reshape(1, channels), w_query, w_key, w_value, w_output,
    )
    half = pl.BlockSpec(
        (1, height // 2, width, channels), lambda i: (lax.div(i, 2), lax.rem(i, 2), 0, 0)
    )
    out_mat, line = sds((rows_each, inner), f32), sds((1, channels), f32)
    out = pl.pallas_call(
        functools.partial(finish_kernel, parts),
        out_shape=[
            sds(latents.shape, f32), sds(conv_kernel.shape, f32), line, line,
            out_mat, out_mat, out_mat, out_mat,
        ],
        grid=(sweeps * 2,),
        in_specs=[half, whole_block(fin.shape), whole_block(small_shape)],
        out_specs=[half] + [
            whole_block(shape)
            for shape in (conv_kernel.shape, line.shape, line.shape) + (out_mat.shape,) * 4
        ],
        compiler_params=pltpu.CompilerParams(vmem_limit_bytes=BIG),
        name="finish",
    )(raw_lat, fin, small)
    grad_latents, grad_kernel, grad_bias, grad_gain, *mats = out
    return (grad_latents, grad_kernel, grad_bias.reshape(channels), grad_gain.reshape(channels), *mats)


def solution(mesh):
    image = P("sweep", None, "azim", None)
    share = P("azim", None)
    return jax.shard_map(
        on_device,
        mesh=mesh,
        in_specs=(image, image) + (P(),) * 7,
        out_specs=(image, P(), P(), P(), share, share, share, share),
        check_vma=False,
    )
```

```python
import functools
import math

import jax
import jax.numpy as jnp
from jax import lax
from jax.experimental import pallas as pl
from jax.experimental.pallas import tpu as pltpu
from jax.sharding import PartitionSpec as P

DH = 64
EPS = 1e-06
LANES = 128
PIX = 16
MESH = pl.DeviceIdType.MESH
VMEM = pl.BlockSpec(memory_space=pltpu.VMEM)
ANY = pl.BlockSpec(memory_space=pl.ANY)
BIG = 56 * 1024 * 1024


def remote(src, dst, send, recv, where):
    return pltpu.make_async_remote_copy(
        src_ref=src, dst_ref=dst, send_sem=send, recv_sem=recv, device_id=where, device_id_type=MESH
    )


def greet(partners):
    barrier = pltpu.get_barrier_semaphore()
    for where in partners:
        pl.semaphore_signal(barrier, inc=1, device_id=where, device_id_type=MESH)
    pl.semaphore_wait(barrier, len(partners))


def store_shifted(dst, s, h, val):
    width = val.shape[0]
    dst[1, s, h + 1] = val
    dst[0, s, h + 1] = pltpu.roll(val, 1, 0)
    dst[2, s, h + 1] = pltpu.roll(val, width - 1, 0)


def patch_edges(dst, left, right, sweeps, height, width):
    for s in range(sweeps):
        for h in range(height):
            i = s * height + h
            dst[0, s, h + 1, 0:1, :] = left[i : i + 1, :]
            dst[2, s, h + 1, width - 1 : width, :] = right[i : i + 1, :]


def zero_frame(dst, sweeps, height):
    for b in range(3):
        for s in range(sweeps):
            dst[b, s, 0] = jnp.zeros(dst.shape[3:], jnp.float32)
            dst[b, s, height + 1] = jnp.zeros(dst.shape[3:], jnp.float32)


def dot(a, b, dims):
    return lax.dot_general(a, b, (dims, ((), ())), preferred_element_type=jnp.float32)


NN = ((1,), (0,))
NT = ((1,), (1,))
TN = ((0,), (0,))


def block_kernel(
    groups, strips, heads, predivide, direct,
    lat, cot, kern, bias, gain_ref, wq_hbm, wk_hbm, wv_hbm, wo_hbm,
    out_lat, out_fin, out_small,
    act, gy, y_src, y_pix, cot_pix, grad, ret,
    fore_left, fore_right, fore_in_left, fore_in_right, edge_left, edge_right, in_left, in_right,
    weights, left_s, right_s, grad_att_s, mats, pair_buf, acc, sweep_buf, sweep_sum, z_buf,
    early_z, early_sum, late_buf, lat_out,
    taps, small, small_pair, small_sweep, small_z,
    w_sem, own_sem, a2a_send, a2a_recv, back_send, back_recv, halo_send, halo_recv,
    pair_send, pair_recv, one_send, one_recv, two_send, two_recv, fin_send, fin_recv,
    sp_send, sp_recv, ss_send, ss_recv, sz_send, sz_recv, lat_sem,
):
    sweeps, height, width, channels = lat.shape
    each = height * width // groups
    planes = strips // 2
    inner = right_s.shape[2]
    me = lax.axis_index("sweep")
    az = lax.axis_index("azim")
    core = lax.rem(az, 2)
    z = az // 2
    other = az + 1 - 2 * core
    right, left = lax.rem(az + 1, strips), lax.rem(az + strips - 1, strips)
    partners = [lax.rem(me + k, groups) for k in range(1, groups)]
    z_partners = [lax.rem(z + k, planes) for k in range(1, planes)]
    pending = []

    def send(*args):
        copy = remote(*args)
        copy.start()
        pending.append(copy)
        return copy

    loads = []
    for i, w in enumerate((wq_hbm, wk_hbm, wv_hbm, wo_hbm)):
        loads.append(pltpu.make_async_copy(w, weights.at[i], w_sem.at[i]))
        loads[-1].start()
    greet(
        [{"sweep": g} for g in partners]
        + [{"azim": left}, {"azim": right}, {"azim": other}]
        + [{"azim": p * 2 + core} for p in z_partners]
    )
    mine = pl.ds(pl.multiple_of(me * each, PIX), each)
    slots = pl.ds(me * sweeps, sweeps)

    for s in range(sweeps):
        for h in range(height):
            i = s * height + h
            fore_left[i : i + 1, :] = lat[s, h, 0:16, :].astype(jnp.float32)[0:1]
            fore_right[i : i + 1, :] = lat[s, h, width - 16 : width, :].astype(jnp.float32)[15:16]
    to_right = send(fore_right, fore_in_left, halo_send.at[0], halo_recv.at[0], {"azim": right})
    to_left = send(fore_left, fore_in_right, halo_send.at[1], halo_recv.at[1], {"azim": left})

    def give(k, g, source, target, stage, count, send_sem, recv_sem):
        there = pl.ds(pl.multiple_of(g * each + stage * count, PIX), count)
        here = slice(stage * count, (stage + 1) * count)
        return send(source.at[:, there, :], target.at[slots, here, :], send_sem, recv_sem, {"sweep": g})

    cot_copies = [give(k, g, cot, cot_pix, 0, each, a2a_send.at[0, k], a2a_recv.at[0, k]) for k, g in enumerate(partners)]
    cot_own = pltpu.make_async_copy(cot.at[:, mine, :], cot_pix.at[slots], own_sem.at[0])
    cot_own.start()

    for s in range(sweeps):
        def activate(h, carry, s=s):
            x = lat[s, h].astype(jnp.float32)
            store_shifted(act, s, h, x / (1.0 + jnp.exp(-x)))
            return carry
        lax.fori_loop(0, height, activate, 0)
    zero_frame(act, sweeps, height)
    zero_frame(gy, sweeps, height)
    taps[...] = jnp.zeros(taps.shape, jnp.float32)
    to_right.wait_recv()
    to_left.wait_recv()
    for ref in (fore_in_left, fore_in_right):
        x = ref[...]
        ref[...] = x / (1.0 + jnp.exp(-x))
    patch_edges(act, fore_in_left, fore_in_right, sweeps, height, width)

    def convolve_row(s, h):
        total = lat[s, h].astype(jnp.float32) + bias[...]
        for a in range(3):
            for b in range(3):
                total = total + kern[3 * a + b : 3 * a + b + 1, :] * act[b, s, h + a]
        y_src[s, pl.ds(pl.multiple_of(h * width, PIX), width), :] = total.astype(jnp.bfloat16)

    lines = height // groups if groups <= height else 1
    count = each // lines
    y_copies = [[] for _ in range(lines)]

    def give_y(k, g, stage):
        y_copies[stage].append(
            give(k, g, y_src, y_pix, stage, count, a2a_send.at[1 + stage, k], a2a_recv.at[1 + stage, k])
        )

    if groups <= height:
        for stage in range(lines):
            for k, g in enumerate(partners + [me]):
                for sweep in range(sweeps):
                    convolve_row(sweep, g * lines + stage)
                if k < groups - 1:
                    give_y(k, g, stage)
    else:
        def whole(i, carry):
            convolve_row(i // height, i % height)
            return carry
        lax.fori_loop(0, sweeps * height, whole, 0)
        for k, g in enumerate(partners):
            give_y(k, g, 0)
    y_own = pltpu.make_async_copy(y_src.at[:, mine, :], y_pix.at[slots], own_sem.at[1])
    y_own.start()

    m = groups * sweeps * PIX
    blocks = each // PIX
    total_sweeps = groups * sweeps
    scale = 1.0 / math.sqrt(DH)
    gain = gain_ref[...]
    for load in loads:
        load.wait()
    for copy in cot_copies:
        copy.wait_recv()
    cot_own.wait()
    for block in range(blocks):
        at = slice(block * PIX, (block + 1) * PIX)
        own = slice(block * m, (block + 1) * m)
        rows = cot_pix[:, at, :].reshape(m, channels)
        left_s[1, own, :] = rows
        grad_att_s[own, :] = dot(rows, weights[3], NN).astype(jnp.bfloat16)
    row_pix = lax.broadcasted_iota(jnp.int32, (m, m), 0) % PIX
    col_pix = lax.broadcasted_iota(jnp.int32, (m, m), 1) % PIX
    same = row_pix == col_pix
    same = jnp.concatenate([same] * heads, axis=0)
    lane_head = lax.broadcasted_iota(jnp.int32, (1, inner), 1) // DH

    def spread(value):
        return jnp.concatenate(
            [jnp.where(lane_head == h, value, jnp.zeros_like(value)) for h in range(heads)], axis=0
        )

    def collect(value):
        total = jnp.where(lane_head == 0, value[0:m], 0.0)
        for h in range(1, heads):
            total = jnp.where(lane_head == h, value[h * m : (h + 1) * m], total)
        return total

    pairs, firsts, seconds, gather = {}, {}, {}, []

    def form(i):
        full = dot(left_s[i // 3], right_s[i], TN)
        if not direct:
            out_fin[i] = full
            return
        _, lanes, _, _, rows, _ = mats.shape
        for j in range(lanes):
            part = full[:, j * LANES : (j + 1) * LANES]
            mats[i, j] = part.reshape(planes, 2, rows, LANES)
        pairs[i] = send(
            mats.at[i, :, :, 1 - core], pair_buf.at[i], pair_send.at[i], pair_recv.at[i], {"azim": other}
        )

    def scatter_first(i):
        if not direct:
            return
        pairs[i].wait_recv()
        _, _, _, lanes, rows, _ = acc.shape
        for q in range(planes):
            for g in range(groups):
                at = slice(g * rows, (g + 1) * rows)
                for j in range(lanes):
                    acc[i, q, g, j] = mats[i, j, q, core, at, :] + pair_buf[i, j, q, at, :]
        firsts[i] = []
        if i == 3:
            for k, p in enumerate(z_partners):
                firsts[i].append(
                    send(acc.at[i, p], early_z.at[k], one_send.at[i, k], one_recv.at[i, k], {"azim": p * 2 + core})
                )
        else:
            for k, g in enumerate(partners):
                firsts[i].append(
                    send(acc.at[i, :, g], sweep_buf.at[i, k], one_send.at[i, k], one_recv.at[i, k], {"sweep": g})
                )

    def scatter_second(i):
        if not direct:
            return
        for copy in firsts[i]:
            copy.wait_recv()
        seconds[i] = []
        if i == 3:
            for k, g in enumerate(partners + [me]):
                total = acc[i, z, g]
                for j in range(planes - 1):
                    total = total + early_z[j, g]
                early_sum[g] = total
                if k < groups - 1:
                    seconds[i].append(
                        send(early_sum.at[g], late_buf.at[k], two_send.at[i, k], two_recv.at[i, k], {"sweep": g})
                    )
        else:
            for k, p in enumerate(z_partners + [z]):
                total = acc[i, p, me]
                for j in range(groups - 1):
                    total = total + sweep_buf[i, j, p]
                sweep_sum[i, p] = total
                if k < planes - 1:
                    seconds[i].append(
                        send(
                            sweep_sum.at[i, p], z_buf.at[i, k], two_send.at[i, k], two_recv.at[i, k],
                            {"azim": p * 2 + core},
                        )
                    )

    def gather_final(i):
        if not direct:
            return
        for copy in seconds[i]:
            copy.wait_recv()
        if i == 3:
            total = early_sum[me]
            for k in range(groups - 1):
                total = total + late_buf[k]
        else:
            total = sweep_sum[i, z]
            for k in range(planes - 1):
                total = total + z_buf[i, k]
        out_fin[me, i] = total * predivide
        for k, g in enumerate(partners):
            some = out_fin.at[me, i]
            gather.append(send(some, some, fin_send.at[i, k], fin_recv.at[i, k], {"sweep": g}))

    y_own.wait()
    back, back_own = [], []
    gain_total = jnp.zeros((1, channels), jnp.float32)
    several = count // PIX
    for stage in range(lines):
        for copy in y_copies[stage]:
            copy.wait_recv()
        base = stage * count
        span = slice(stage * several * m, (stage + 1) * several * m)
        y = jnp.concatenate(
            [
                y_pix[:, base + i * PIX : base + (i + 1) * PIX, :].reshape(m, channels)
                for i in range(several)
            ],
            axis=0,
        ).astype(jnp.float32)
        root = jnp.sqrt(jnp.mean(y * y, axis=-1, keepdims=True) + EPS)
        inverse = 1.0 / root
        normed = (y * inverse * gain).astype(jnp.bfloat16)
        left_s[0, span, :] = normed
        queries = dot(normed, weights[0], NN).astype(jnp.bfloat16)
        keys = dot(normed, weights[1], NN).astype(jnp.bfloat16)
        values = dot(normed, weights[2], NN).astype(jnp.bfloat16)
        forward = []
        for i in range(several):
            part = slice(i * m, (i + 1) * m)
            own = slice((stage * several + i) * m, (stage * several + i + 1) * m)
            key, value = keys[part], values[part]
            query_x = spread(queries[part])
            grad_att_x = spread(grad_att_s[own, :])
            scores = jnp.where(same, dot(query_x, key, NT) * scale, -1e30)
            top = jnp.max(scores, axis=-1, keepdims=True)
            expon = jnp.exp(scores - top)
            probs = expon / jnp.sum(expon, axis=-1, keepdims=True)
            probs_low = probs.astype(jnp.bfloat16)
            right_s[3, own, :] = collect(dot(probs_low, value, NN)).astype(jnp.bfloat16)
            grad_v = dot(probs_low, grad_att_x, TN).astype(jnp.bfloat16)
            right_s[2, own, :] = grad_v
            forward.append((own, key, value, query_x, grad_att_x, probs, grad_v))
        last = stage == lines - 1
        if last:
            form(3)
            form(2)
            scatter_first(3)
        grads = []
        for own, key, value, query_x, grad_att_x, probs, grad_v in forward:
            grad_probs = dot(grad_att_x, value, NT)
            inner_sum = jnp.sum(probs * grad_probs, axis=-1, keepdims=True)
            grad_scores = (probs * (grad_probs - inner_sum) * scale).astype(jnp.bfloat16)
            grad_q = collect(dot(grad_scores, key, NN)).astype(jnp.bfloat16)
            grad_k = dot(grad_scores, query_x, TN).astype(jnp.bfloat16)
            right_s[0, own, :] = grad_q
            right_s[1, own, :] = grad_k
            grads.append((grad_q, grad_k, grad_v))
        if last:
            scatter_first(2)
            form(0)
            form(1)
        grad_q, grad_k, grad_v = (jnp.concatenate(each_grad, axis=0) for each_grad in zip(*grads))
        grad_normed = (
            dot(grad_q, weights[0], NT) + dot(grad_k, weights[1], NT) + dot(grad_v, weights[2], NT)
        )
        gain_total = gain_total + jnp.sum(grad_normed * y * inverse, axis=0, keepdims=True)
        gained = grad_normed * gain
        mean = jnp.mean(gained * y, axis=-1, keepdims=True)
        grad_attn = (inverse * (gained - y * mean * inverse * inverse)).astype(jnp.bfloat16)
        for i in range(several):
            at = slice(base + i * PIX, base + (i + 1) * PIX)
            grad[:, at, :] = grad_attn[i * m : (i + 1) * m].reshape(total_sweeps, PIX, channels)
        at = slice(base, base + count)
        here = pl.ds(pl.multiple_of(me * each + base, PIX), count)
        for k, g in enumerate(partners):
            back.append(
                send(
                    grad.at[pl.ds(g * sweeps, sweeps), at, :], ret.at[:, here, :],
                    back_send.at[stage, k], back_recv.at[stage, k], {"sweep": g},
                )
            )
        back_own.append(
            pltpu.make_async_copy(grad.at[slots, at, :], ret.at[:, here, :], own_sem.at[2 + stage])
        )
        back_own[-1].start()

    scatter_first(0)
    scatter_first(1)

    for copy in back:
        copy.wait_recv()
    for copy in back_own:
        copy.wait()
    for s in range(sweeps):
        def combine(h, carry, s=s):
            at = pl.ds(pl.multiple_of(h * width, PIX), width)
            val = cot[s, at, :].astype(jnp.float32) + ret[s, at, :].astype(jnp.float32)
            store_shifted(gy, s, h, val)
            edge_left[pl.ds(s * height + h, 1), :] = val[0:1]
            edge_right[pl.ds(s * height + h, 1), :] = val[width - 1 : width]
            return carry
        lax.fori_loop(0, height, combine, 0)
    to_right = send(edge_right, in_left, halo_send.at[2], halo_recv.at[2], {"azim": right})
    to_left = send(edge_left, in_right, halo_send.at[3], halo_recv.at[3], {"azim": left})

    scatter_second(2)

    def fold(v):
        return sum(v[8 * i : 8 * i + 8] for i in range(1, width // 8)) + v[0:8]

    for s in range(sweeps):
        def weigh(h, carry, s=s):
            mid = gy[1, s, h + 1]
            for t in range(9):
                taps[t] = taps[t] + fold(mid * act[t % 3, s, h + t // 3])
            taps[9] = taps[9] + fold(mid)
            return carry
        lax.fori_loop(0, height, weigh, 0)
    small[...] = jnp.zeros(small.shape, jnp.float32)
    for t in range(10):
        small[t : t + 1, :] = jnp.sum(taps[t], axis=0, keepdims=True) * predivide
    small[10:11, :] = gain_total * predivide
    sp = send(small, small_pair, sp_send, sp_recv, {"azim": other})

    scatter_second(3)
    to_right.wait_recv()
    to_left.wait_recv()
    patch_edges(gy, in_left, in_right, sweeps, height, width)
    for s in range(sweeps):
        def convolve(h, carry, s=s):
            mid = gy[1, s, h + 1]
            total = jnp.zeros(mid.shape, jnp.float32)
            for a in range(3):
                for b in range(3):
                    t = 3 * a + b
                    total = total + kern[t : t + 1, :] * gy[2 - b, s, h + 2 - a]
            x = lat[s, h].astype(jnp.float32)
            sig = 1.0 / (1.0 + jnp.exp(-x))
            lat_out[s, h] = mid + total * (sig * (1.0 + x * (1.0 - sig)))
            return carry
        lax.fori_loop(0, height, convolve, 0)
    lat_copy = pltpu.make_async_copy(lat_out, out_lat, lat_sem)
    lat_copy.start()

    scatter_second(0)
    gather_final(3)
    sp.wait_recv()
    small_sweep[me] = small[...] + small_pair[...]
    ss = []
    for k, g in enumerate(partners):
        ss.append(
            send(small_sweep.at[me], small_sweep.at[me], ss_send.at[k], ss_recv.at[k], {"sweep": g})
        )

    scatter_second(1)
    gather_final(2)
    for copy in ss:
        copy.wait_recv()
    total = small_sweep[0]
    for g in range(1, groups):
        total = total + small_sweep[g]
    small_z[z] = total
    sz = []
    for k, p in enumerate(z_partners):
        sz.append(
            send(small_z.at[z], small_z.at[z], sz_send.at[k], sz_recv.at[k], {"azim": p * 2 + core})
        )

    gather_final(0)
    gather_final(1)
    for copy in sz:
        copy.wait_recv()
    total = small_z[0]
    for p in range(1, planes):
        total = total + small_z[p]
    out_small[...] = total
    for copy in gather:
        copy.wait_recv()
    for copy in pending:
        copy.wait_send()
    lat_copy.wait()


def finish_kernel(lat, fin, small, out_lat, out_kern, out_bias, out_gain, out_q, out_k, out_v, out_o):
    out_lat[...] = lat[...]

    @pl.when(pl.program_id(0) == 0)
    def unpack():
        for i, out in enumerate((out_q, out_k, out_v, out_o)):
            if len(fin.shape) == 3:
                out[...] = fin[i]
            else:
                groups, _, lanes, rows, _ = fin.shape
                for g in range(groups):
                    for j in range(lanes):
                        out[g * rows : (g + 1) * rows, j * LANES : (j + 1) * LANES] = fin[g, i, j]
        out_kern[...] = small[0:9, :]
        out_bias[...] = small[9:10, :]
        out_gain[...] = small[10:11, :]


def whole_block(shape):
    return pl.BlockSpec(shape, lambda i: (0,) * len(shape))


def on_device(
    latents, cotangent, conv_kernel, conv_bias, norm_gain, w_query, w_key, w_value, w_output
):
    f32, bf16 = jnp.float32, jnp.bfloat16
    dma = pltpu.SemaphoreType.DMA
    sds = jax.ShapeDtypeStruct
    sweeps, height, width, channels = latents.shape
    inner = w_query.shape[1]
    groups = lax.axis_size("sweep")
    strips = lax.axis_size("azim")
    planes = strips // 2
    each = height * width // groups
    total = sweeps * groups
    tokens = total * each
    edge = pltpu.VMEM((sweeps * height, channels), f32)
    framed = pltpu.VMEM((3, sweeps, height + 2, width, channels), f32)
    flat = (sweeps, height * width, channels)
    pixels = pltpu.VMEM((total, each, channels), bf16)
    lanes = inner // LANES
    rows_each = channels // strips
    direct = rows_each % (8 * groups) == 0
    rows = rows_each // groups if direct else 8
    fin_shape = (groups, 4, lanes, rows, LANES) if direct else (4, channels, inner)
    share = (lanes, rows, LANES)
    most = max(groups, planes) - 1
    predivide = 1.0 / math.sqrt(total * height * width * strips)
    small_shape = (16, channels)
    lines = height // groups if groups <= height else 1
    to_sweep, to_z, one = dma((groups - 1,)), dma((planes - 1,)), dma(())

    raw_lat, fin, small = pl.pallas_call(
        functools.partial(block_kernel, groups, strips, inner // DH, predivide, direct),
        out_shape=[
            sds(latents.shape, f32), sds(fin_shape, f32), sds(small_shape, f32),
        ],
        in_specs=[VMEM] * 5 + [ANY] * 4,
        out_specs=[ANY, VMEM, VMEM],
        scratch_shapes=[
            framed, framed, pltpu.VMEM(flat, bf16), pixels, pixels, pixels, pltpu.VMEM(flat, bf16),
            edge, edge, edge, edge, edge, edge, edge, edge,
            pltpu.VMEM((4, channels, inner), bf16),
            pltpu.VMEM((2, tokens, channels), bf16),
            pltpu.VMEM((4, tokens, inner), bf16),
            pltpu.VMEM((tokens, inner), bf16),
            pltpu.VMEM((4, lanes, planes, 2, groups * rows, LANES), f32),
            pltpu.VMEM((4, lanes, planes, groups * rows, LANES), f32),
            pltpu.VMEM((4, planes, groups) + share, f32),
            pltpu.VMEM((3, groups - 1, planes) + share, f32),
            pltpu.VMEM((3, planes) + share, f32),
            pltpu.VMEM((3, planes - 1) + share, f32),
            pltpu.VMEM((planes - 1, groups) + share, f32),
            pltpu.VMEM((groups,) + share, f32),
            pltpu.VMEM((groups - 1,) + share, f32),
            pltpu.VMEM(latents.shape, f32),
            pltpu.VMEM((10, 8, channels), f32),
            pltpu.VMEM(small_shape, f32),
            pltpu.VMEM(small_shape, f32),
            pltpu.VMEM((groups,) + small_shape, f32),
            pltpu.VMEM((planes,) + small_shape, f32),
            dma((4,)), dma((2 + lines,)), dma((1 + lines, groups - 1)), dma((1 + lines, groups - 1)),
            dma((lines, groups - 1)), dma((lines, groups - 1)), dma((4,)), dma((4,)),
            dma((4,)), dma((4,)), dma((4, most)), dma((4, most)), dma((4, most)), dma((4, most)),
            dma((4, groups - 1)), dma((4, groups - 1)),
            one, one, to_sweep, to_sweep, to_z, to_z, one,
        ],
        compiler_params=pltpu.CompilerParams(
            collective_id=0, has_side_effects=True, vmem_limit_bytes=BIG
        ),
        name="block",
    )(
        latents, cotangent.reshape(flat), conv_kernel, conv_bias.reshape(1, channels),
        norm_gain.reshape(1, channels), w_query, w_key, w_value, w_output,
    )
    if not direct:
        fin = lax.psum_scatter(fin * predivide, "azim", scatter_dimension=1, tiled=True)
        fin = lax.psum(fin, "sweep")
    half = pl.BlockSpec(
        (1, height // 2, width, channels), lambda i: (lax.div(i, 2), lax.rem(i, 2), 0, 0)
    )
    out_mat, line = sds((rows_each, inner), f32), sds((1, channels), f32)
    out = pl.pallas_call(
        finish_kernel,
        out_shape=[
            sds(latents.shape, f32), sds(conv_kernel.shape, f32), line, line,
            out_mat, out_mat, out_mat, out_mat,
        ],
        grid=(sweeps * 2,),
        in_specs=[half, whole_block(fin.shape), whole_block(small_shape)],
        out_specs=[half] + [
            whole_block(shape)
            for shape in (conv_kernel.shape, line.shape, line.shape) + (out_mat.shape,) * 4
        ],
        compiler_params=pltpu.CompilerParams(vmem_limit_bytes=BIG),
        name="finish",
    )(raw_lat, fin, small)
    grad_latents, grad_kernel, grad_bias, grad_gain, *mats = out
    return (grad_latents, grad_kernel, grad_bias.reshape(channels), grad_gain.reshape(channels), *mats)


def solution(mesh):
    image = P("sweep", None, "azim", None)
    share = P("azim", None)
    return jax.shard_map(
        on_device,
        mesh=mesh,
        in_specs=(image, image) + (P(),) * 7,
        out_specs=(image, P(), P(), P(), share, share, share, share),
        check_vma=False,
    )
```

```python
import functools
import math

import jax
import jax.numpy as jnp
from jax import lax
from jax.experimental import pallas as pl
from jax.experimental.pallas import tpu as pltpu
from jax.sharding import PartitionSpec as P

DH = 64
EPS = 1e-06
LANES = 128
PIX = 16
MESH = pl.DeviceIdType.MESH
VMEM = pl.BlockSpec(memory_space=pltpu.VMEM)
ANY = pl.BlockSpec(memory_space=pl.ANY)
BIG = 56 * 1024 * 1024


def remote(src, dst, send, recv, where):
    return pltpu.make_async_remote_copy(
        src_ref=src, dst_ref=dst, send_sem=send, recv_sem=recv, device_id=where, device_id_type=MESH
    )


def greet(partners):
    barrier = pltpu.get_barrier_semaphore()
    for where in partners:
        pl.semaphore_signal(barrier, inc=1, device_id=where, device_id_type=MESH)


def await_greetings(count):
    pl.semaphore_wait(pltpu.get_barrier_semaphore(), count)


def store_shifted(dst, s, h, val):
    width = val.shape[0]
    dst[1, s, h + 1] = val
    dst[0, s, h + 1] = pltpu.roll(val, 1, 0)
    dst[2, s, h + 1] = pltpu.roll(val, width - 1, 0)


def patch_edges(dst, left, right, sweeps, height, width):
    for s in range(sweeps):
        for h in range(height):
            i = s * height + h
            dst[0, s, h + 1, 0:1, :] = left[i : i + 1, :]
            dst[2, s, h + 1, width - 1 : width, :] = right[i : i + 1, :]


def zero_frame(dst, sweeps, height):
    for b in range(3):
        for s in range(sweeps):
            dst[b, s, 0] = jnp.zeros(dst.shape[3:], jnp.float32)
            dst[b, s, height + 1] = jnp.zeros(dst.shape[3:], jnp.float32)


def dot(a, b, dims):
    return lax.dot_general(a, b, (dims, ((), ())), preferred_element_type=jnp.float32)


NN = ((1,), (0,))
NT = ((1,), (1,))
TN = ((0,), (0,))


def block_kernel(
    groups, strips, heads, predivide,
    lat_hbm, cot_hbm, kern_hbm, bias_hbm, gain_hbm, wq_hbm, wk_hbm, wv_hbm, wo_hbm,
    out_lat, out_fin, out_small,
    lat, cot, kern, bias, gain_ref, act, gy, y_src, y_pix, cot_pix, grad, ret,
    fore_left, fore_right, fore_in_left, fore_in_right, edge_left, edge_right, in_left, in_right,
    weights, left_s, right_s, grad_att_s, mats, pair_buf, acc, sweep_buf, acc2, z_buf, early_z, early_sum, late_buf, lat_out,
    taps, small, small_pair, small_sweep, small_z,
    w_sem, own_sem, a2a_send, a2a_recv, back_send, back_recv, halo_send, halo_recv,
    pair_send, pair_recv, sweep_send, sweep_recv, z_send, z_recv, fin_send, fin_recv,
    sp_send, sp_recv, ss_send, ss_recv, sz_send, sz_recv, lat_sem, in_sem, ez_send, ez_recv, late_send, late_recv,
):
    sweeps, height, width, channels = lat.shape
    each = height * width // groups
    planes = strips // 2
    inner = right_s.shape[2]
    me = lax.axis_index("sweep")
    az = lax.axis_index("azim")
    core = lax.rem(az, 2)
    z = az // 2
    other = az + 1 - 2 * core
    right, left = lax.rem(az + 1, strips), lax.rem(az + strips - 1, strips)
    partners = [lax.rem(me + k, groups) for k in range(1, groups)]
    z_partners = [lax.rem(z + k, planes) for k in range(1, planes)]
    pending = []

    def send(*args):
        copy = remote(*args)
        copy.start()
        pending.append(copy)
        return copy

    greetings = (
        [{"sweep": g} for g in partners]
        + [{"azim": left}, {"azim": right}, {"azim": other}]
        + [{"azim": p * 2 + core} for p in z_partners]
    )
    greet(greetings)
    inputs = []
    for i, (source, target) in enumerate(
        ((lat_hbm, lat), (cot_hbm, cot), (kern_hbm, kern), (bias_hbm, bias), (gain_hbm, gain_ref))
    ):
        inputs.append(pltpu.make_async_copy(source, target, in_sem.at[i]))
        inputs[-1].start()
    loads = []
    for i, w in enumerate((wq_hbm, wk_hbm, wv_hbm, wo_hbm)):
        loads.append(pltpu.make_async_copy(w, weights.at[i], w_sem.at[i]))
        loads[-1].start()
    mine = pl.ds(pl.multiple_of(me * each, PIX), each)
    slots = pl.ds(me * sweeps, sweeps)

    inputs[0].wait()
    for s in range(sweeps):
        for h in range(height):
            i = s * height + h
            fore_left[i : i + 1, :] = lat[s, h, 0:16, :].astype(jnp.float32)[0:1]
            fore_right[i : i + 1, :] = lat[s, h, width - 16 : width, :].astype(jnp.float32)[15:16]
    await_greetings(len(greetings))
    to_right = send(fore_right, fore_in_left, halo_send.at[0], halo_recv.at[0], {"azim": right})
    to_left = send(fore_left, fore_in_right, halo_send.at[1], halo_recv.at[1], {"azim": left})

    def give(k, g, source, target, stage, count, send_sem, recv_sem):
        there = pl.ds(pl.multiple_of(g * each + stage * count, PIX), count)
        here = slice(stage * count, (stage + 1) * count)
        return send(source.at[:, there, :], target.at[slots, here, :], send_sem, recv_sem, {"sweep": g})

    inputs[1].wait()
    cot_copies = [give(k, g, cot, cot_pix, 0, each, a2a_send.at[0, k], a2a_recv.at[0, k]) for k, g in enumerate(partners)]
    cot_own = pltpu.make_async_copy(cot.at[:, mine, :], cot_pix.at[slots], own_sem.at[0])
    cot_own.start()

    for copy in inputs[2:]:
        copy.wait()
    for s in range(sweeps):
        def activate(h, carry, s=s):
            x = lat[s, h].astype(jnp.float32)
            store_shifted(act, s, h, x / (1.0 + jnp.exp(-x)))
            return carry
        lax.fori_loop(0, height, activate, 0)
    zero_frame(act, sweeps, height)
    zero_frame(gy, sweeps, height)
    taps[...] = jnp.zeros(taps.shape, jnp.float32)
    to_right.wait_recv()
    to_left.wait_recv()
    for ref in (fore_in_left, fore_in_right):
        x = ref[...]
        ref[...] = x / (1.0 + jnp.exp(-x))
    patch_edges(act, fore_in_left, fore_in_right, sweeps, height, width)

    def convolve_row(s, h):
        total = lat[s, h].astype(jnp.float32) + bias[...]
        for a in range(3):
            for b in range(3):
                total = total + kern[3 * a + b : 3 * a + b + 1, :] * act[b, s, h + a]
        y_src[s, pl.ds(pl.multiple_of(h * width, PIX), width), :] = total.astype(jnp.bfloat16)

    lines = height // groups if groups <= height else 1
    count = each // lines
    y_copies = [[] for _ in range(lines)]

    def give_y(k, g, stage):
        y_copies[stage].append(
            give(k, g, y_src, y_pix, stage, count, a2a_send.at[1 + stage, k], a2a_recv.at[1 + stage, k])
        )

    if groups <= height:
        for stage in range(lines):
            for k, g in enumerate(partners + [me]):
                for sweep in range(sweeps):
                    convolve_row(sweep, g * lines + stage)
                if k < groups - 1:
                    give_y(k, g, stage)
    else:
        def whole(i, carry):
            convolve_row(i // height, i % height)
            return carry
        lax.fori_loop(0, sweeps * height, whole, 0)
        for k, g in enumerate(partners):
            give_y(k, g, 0)
    y_own = pltpu.make_async_copy(y_src.at[:, mine, :], y_pix.at[slots], own_sem.at[1])
    y_own.start()

    m = groups * sweeps * PIX
    blocks = each // PIX
    total_sweeps = groups * sweeps
    scale = 1.0 / math.sqrt(DH)
    gain = gain_ref[...]
    for load in loads:
        load.wait()
    for copy in cot_copies:
        copy.wait_recv()
    cot_own.wait()
    for block in range(blocks):
        at = slice(block * PIX, (block + 1) * PIX)
        own = slice(block * m, (block + 1) * m)
        rows = cot_pix[:, at, :].reshape(m, channels)
        left_s[1, own, :] = rows
        grad_att_s[own, :] = dot(rows, weights[3], NN).astype(jnp.bfloat16)
    row_pix = lax.broadcasted_iota(jnp.int32, (m, m), 0) % PIX
    col_pix = lax.broadcasted_iota(jnp.int32, (m, m), 1) % PIX
    same = row_pix == col_pix
    same = jnp.concatenate([same] * heads, axis=0)
    lane_head = lax.broadcasted_iota(jnp.int32, (1, inner), 1) // DH

    def spread(value):
        return jnp.concatenate(
            [jnp.where(lane_head == h, value, jnp.zeros_like(value)) for h in range(heads)], axis=0
        )

    def collect(value):
        total = jnp.where(lane_head == 0, value[0:m], 0.0)
        for h in range(1, heads):
            total = jnp.where(lane_head == h, value[h * m : (h + 1) * m], total)
        return total

    y_own.wait()
    back, back_own = [], []
    gain_total = jnp.zeros((1, channels), jnp.float32)
    several = count // PIX
    for stage in range(lines):
        for copy in y_copies[stage]:
            copy.wait_recv()
        base = stage * count
        span = slice(stage * several * m, (stage + 1) * several * m)
        y = jnp.concatenate(
            [
                y_pix[:, base + i * PIX : base + (i + 1) * PIX, :].reshape(m, channels)
                for i in range(several)
            ],
            axis=0,
        ).astype(jnp.float32)
        root = jnp.sqrt(jnp.mean(y * y, axis=-1, keepdims=True) + EPS)
        inverse = 1.0 / root
        normed = (y * inverse * gain).astype(jnp.bfloat16)
        left_s[0, span, :] = normed
        queries = dot(normed, weights[0], NN).astype(jnp.bfloat16)
        keys = dot(normed, weights[1], NN).astype(jnp.bfloat16)
        values = dot(normed, weights[2], NN).astype(jnp.bfloat16)
        grads = []
        for i in range(several):
            part = slice(i * m, (i + 1) * m)
            own = slice((stage * several + i) * m, (stage * several + i + 1) * m)
            key, value = keys[part], values[part]
            query_x = spread(queries[part])
            grad_att_x = spread(grad_att_s[own, :])
            scores = jnp.where(same, dot(query_x, key, NT) * scale, -1e30)
            top = jnp.max(scores, axis=-1, keepdims=True)
            expon = jnp.exp(scores - top)
            probs = expon / jnp.sum(expon, axis=-1, keepdims=True)
            probs_low = probs.astype(jnp.bfloat16)
            right_s[3, own, :] = collect(dot(probs_low, value, NN)).astype(jnp.bfloat16)
            grad_probs = dot(grad_att_x, value, NT)
            inner_sum = jnp.sum(probs * grad_probs, axis=-1, keepdims=True)
            grad_scores = (probs * (grad_probs - inner_sum) * scale).astype(jnp.bfloat16)
            grad_v = dot(probs_low, grad_att_x, TN).astype(jnp.bfloat16)
            grad_q = collect(dot(grad_scores, key, NN)).astype(jnp.bfloat16)
            grad_k = dot(grad_scores, query_x, TN).astype(jnp.bfloat16)
            right_s[0, own, :] = grad_q
            right_s[1, own, :] = grad_k
            right_s[2, own, :] = grad_v
            grads.append((grad_q, grad_k, grad_v))
        grad_q, grad_k, grad_v = (jnp.concatenate(each_grad, axis=0) for each_grad in zip(*grads))
        grad_normed = (
            dot(grad_q, weights[0], NT) + dot(grad_k, weights[1], NT) + dot(grad_v, weights[2], NT)
        )
        gain_total = gain_total + jnp.sum(grad_normed * y * inverse, axis=0, keepdims=True)
        gained = grad_normed * gain
        mean = jnp.mean(gained * y, axis=-1, keepdims=True)
        grad_attn = (inverse * (gained - y * mean * inverse * inverse)).astype(jnp.bfloat16)
        for i in range(several):
            at = slice(base + i * PIX, base + (i + 1) * PIX)
            grad[:, at, :] = grad_attn[i * m : (i + 1) * m].reshape(total_sweeps, PIX, channels)
        at = slice(base, base + count)
        here = pl.ds(pl.multiple_of(me * each + base, PIX), count)
        for k, g in enumerate(partners):
            back.append(
                send(
                    grad.at[pl.ds(g * sweeps, sweeps), at, :], ret.at[:, here, :],
                    back_send.at[stage, k], back_recv.at[stage, k], {"sweep": g},
                )
            )
        back_own.append(
            pltpu.make_async_copy(grad.at[slots, at, :], ret.at[:, here, :], own_sem.at[2 + stage])
        )
        back_own[-1].start()

    _, lanes, _, _, parts, rows, _ = mats.shape
    per = 4 * lanes * parts // groups
    interleave = groups == 4
    order = [lax.rem(me + k + 1, 4) if interleave else k for k in range(4)]
    scatter, early = [], []
    units = lanes * parts
    split = rows - rows * 3 // 8 // 8 * 8

    def scatter_to(k, g):
        scatter.append(
            send(acc.at[pl.ds(g * per, per), :, 0:split], sweep_buf.at[k], sweep_send.at[k], sweep_recv.at[k], {"sweep": g})
        )

    pairs = []

    def form(n):
        i = order[n]
        full = dot(left_s[i // 3], right_s[i], TN)
        for j in range(lanes):
            part = full[:, j * LANES : (j + 1) * LANES]
            mats[i, j] = part.reshape(planes, 2, parts, rows, LANES)
        pairs.append(
            send(mats.at[i, :, :, 1 - core], pair_buf.at[i], pair_send.at[n], pair_recv.at[n], {"azim": other})
        )

    form(0)
    form(1)
    for n, i in enumerate(order):
        if n + 2 < 4:
            form(n + 2)
        pairs[n].wait_recv()
        for j in range(lanes):
            for p in range(parts):
                for q in range(planes):
                    acc[(i * lanes + j) * parts + p, q] = mats[i, j, q, core, p] + pair_buf[i, j, q, p]
        if interleave and n < 3:
            scatter_to(n, i)
        if split < rows:
            of = pl.ds(i * units, units)
            for k, p in enumerate(z_partners):
                early.append(
                    send(
                        acc.at[of, p, split:rows], early_z.at[k, of], ez_send.at[n, k], ez_recv.at[n, k],
                        {"azim": p * 2 + core},
                    )
                )
    if not interleave:
        for k, g in enumerate(partners):
            scatter_to(k, g)

    for copy in back:
        copy.wait_recv()
    for copy in back_own:
        copy.wait()
    for s in range(sweeps):
        def combine(h, carry, s=s):
            at = pl.ds(pl.multiple_of(h * width, PIX), width)
            val = cot[s, at, :].astype(jnp.float32) + ret[s, at, :].astype(jnp.float32)
            store_shifted(gy, s, h, val)
            edge_left[pl.ds(s * height + h, 1), :] = val[0:1]
            edge_right[pl.ds(s * height + h, 1), :] = val[width - 1 : width]
            return carry
        lax.fori_loop(0, height, combine, 0)
    to_right = send(edge_right, in_left, halo_send.at[2], halo_recv.at[2], {"azim": right})
    to_left = send(edge_left, in_right, halo_send.at[3], halo_recv.at[3], {"azim": left})

    def fold(v):
        return sum(v[8 * i : 8 * i + 8] for i in range(1, width // 8)) + v[0:8]

    for s in range(sweeps):
        def weigh(h, carry, s=s):
            mid = gy[1, s, h + 1]
            for t in range(9):
                taps[t] = taps[t] + fold(mid * act[t % 3, s, h + t // 3])
            taps[9] = taps[9] + fold(mid)
            return carry
        lax.fori_loop(0, height, weigh, 0)
    small[...] = jnp.zeros(small.shape, jnp.float32)
    for t in range(10):
        small[t : t + 1, :] = jnp.sum(taps[t], axis=0, keepdims=True) * predivide
    small[10:11, :] = gain_total * predivide
    sp = send(small, small_pair, sp_send, sp_recv, {"azim": other})

    late = []
    if split < rows:
        for copy in early:
            copy.wait_recv()
        for k, g in enumerate(partners + [me]):
            for i in range(per):
                u = g * per + i
                total = acc[u, z, split:rows]
                for j in range(planes - 1):
                    total = total + early_z[j, u]
                early_sum[u] = total
            if k < groups - 1:
                late.append(
                    send(
                        early_sum.at[pl.ds(g * per, per)], late_buf.at[k], late_send.at[k], late_recv.at[k],
                        {"sweep": g},
                    )
                )
    for copy in scatter:
        copy.wait_recv()
    along = []
    for k, p in enumerate(z_partners + [z]):
        for i in range(per):
            total = acc[me * per + i, p, 0:split]
            for j in range(groups - 1):
                total = total + sweep_buf[j, i, p]
            acc2[p, i] = total
        if k < planes - 1:
            along.append(
                send(acc2.at[p], z_buf.at[k], z_send.at[k], z_recv.at[k], {"azim": p * 2 + core})
            )

    sp.wait_recv()
    small_sweep[me] = small[...] + small_pair[...]
    ss = []
    for k, g in enumerate(partners):
        ss.append(
            send(small_sweep.at[me], small_sweep.at[me], ss_send.at[k], ss_recv.at[k], {"sweep": g})
        )

    to_right.wait_recv()
    to_left.wait_recv()
    patch_edges(gy, in_left, in_right, sweeps, height, width)
    for s in range(sweeps):
        def convolve(h, carry, s=s):
            mid = gy[1, s, h + 1]
            total = jnp.zeros(mid.shape, jnp.float32)
            for a in range(3):
                for b in range(3):
                    t = 3 * a + b
                    total = total + kern[t : t + 1, :] * gy[2 - b, s, h + 2 - a]
            x = lat[s, h].astype(jnp.float32)
            sig = 1.0 / (1.0 + jnp.exp(-x))
            lat_out[s, h] = mid + total * (sig * (1.0 + x * (1.0 - sig)))
            return carry
        lax.fori_loop(0, height, convolve, 0)
    lat_copy = pltpu.make_async_copy(lat_out, out_lat, lat_sem)
    lat_copy.start()

    for copy in ss:
        copy.wait_recv()
    total = small_sweep[0]
    for g in range(1, groups):
        total = total + small_sweep[g]
    small_z[z] = total
    sz = []
    for k, p in enumerate(z_partners):
        sz.append(
            send(small_z.at[z], small_z.at[z], sz_send.at[k], sz_recv.at[k], {"azim": p * 2 + core})
        )

    gather = []
    if split < rows:
        for copy in late:
            copy.wait_recv()
        for i in range(per):
            total = early_sum[me * per + i]
            for k in range(groups - 1):
                total = total + late_buf[k, i]
            out_fin[me, i, split:rows] = total * predivide
        for k, g in enumerate(partners):
            some = out_fin.at[me, :, split:rows]
            gather.append(send(some, some, fin_send.at[1, k], fin_recv.at[1, k], {"sweep": g}))
    for copy in along:
        copy.wait_recv()
    for i in range(per):
        total = acc2[z, i]
        for k in range(planes - 1):
            total = total + z_buf[k, i]
        out_fin[me, i, 0:split] = total * predivide
    for k, g in enumerate(partners):
        some = out_fin.at[me, :, 0:split]
        gather.append(send(some, some, fin_send.at[0, k], fin_recv.at[0, k], {"sweep": g}))
    for copy in sz:
        copy.wait_recv()
    total = small_z[0]
    for p in range(1, planes):
        total = total + small_z[p]
    out_small[...] = total
    for copy in gather:
        copy.wait_recv()
    for copy in pending:
        copy.wait_send()
    lat_copy.wait()


def finish_kernel(parts, lat, fin, small, out_lat, out_kern, out_bias, out_gain, out_q, out_k, out_v, out_o):
    out_lat[...] = lat[...]

    @pl.when(pl.program_id(0) == 0)
    def unpack():
        groups, per, rows, _ = fin.shape
        lanes = groups * per // parts // 4
        for g in range(groups):
            for i in range(per):
                c, p = divmod(g * per + i, parts)
                out = (out_q, out_k, out_v, out_o)[c // lanes]
                j = c % lanes
                out[p * rows : (p + 1) * rows, j * LANES : (j + 1) * LANES] = fin[g, i]
        out_kern[...] = small[0:9, :]
        out_bias[...] = small[9:10, :]
        out_gain[...] = small[10:11, :]


def whole_block(shape):
    return pl.BlockSpec(shape, lambda i: (0,) * len(shape))


def on_device(
    latents, cotangent, conv_kernel, conv_bias, norm_gain, w_query, w_key, w_value, w_output
):
    f32, bf16 = jnp.float32, jnp.bfloat16
    dma = pltpu.SemaphoreType.DMA
    sds = jax.ShapeDtypeStruct
    sweeps, height, width, channels = latents.shape
    inner = w_query.shape[1]
    groups = lax.axis_size("sweep")
    strips = lax.axis_size("azim")
    planes = strips // 2
    each = height * width // groups
    total = sweeps * groups
    tokens = total * each
    edge = pltpu.VMEM((sweeps * height, channels), f32)
    framed = pltpu.VMEM((3, sweeps, height + 2, width, channels), f32)
    flat = (sweeps, height * width, channels)
    pixels = pltpu.VMEM((total, each, channels), bf16)
    lanes = inner // LANES
    chunks = 4 * lanes
    rows_each = channels // strips
    parts = max(1, groups // chunks)
    rows = rows_each // parts
    per = chunks * parts // groups
    predivide = 1.0 / math.sqrt(total * height * width * strips)
    small_shape = (16, channels)
    lines = height // groups if groups <= height else 1
    second = rows * 3 // 8 // 8 * 8
    to_sweep, to_z, one = dma((groups - 1,)), dma((planes - 1,)), dma(())

    raw_lat, fin, small = pl.pallas_call(
        functools.partial(block_kernel, groups, strips, inner // DH, predivide),
        out_shape=[
            sds(latents.shape, f32), sds((groups, per, rows, LANES), f32), sds(small_shape, f32),
        ],
        in_specs=[ANY] * 9,
        out_specs=[ANY, VMEM, VMEM],
        scratch_shapes=[
            pltpu.VMEM(latents.shape, bf16), pltpu.VMEM(flat, bf16), pltpu.VMEM(conv_kernel.shape, f32),
            pltpu.VMEM((1, channels), f32), pltpu.VMEM((1, channels), f32),
            framed, framed, pltpu.VMEM(flat, bf16), pixels, pixels, pixels, pltpu.VMEM(flat, bf16),
            edge, edge, edge, edge, edge, edge, edge, edge,
            pltpu.VMEM((4, channels, inner), bf16),
            pltpu.VMEM((2, tokens, channels), bf16),
            pltpu.VMEM((4, tokens, inner), bf16),
            pltpu.VMEM((tokens, inner), bf16),
            pltpu.VMEM((4, lanes, planes, 2, parts, rows, LANES), f32),
            pltpu.VMEM((4, lanes, planes, parts, rows, LANES), f32),
            pltpu.VMEM((chunks * parts, planes, rows, LANES), f32),
            pltpu.VMEM((groups - 1, per, planes, rows - second, LANES), f32),
            pltpu.VMEM((planes, per, rows - second, LANES), f32),
            pltpu.VMEM((planes - 1, per, rows - second, LANES), f32),
            pltpu.VMEM((planes - 1, chunks * parts, max(8, second), LANES), f32),
            pltpu.VMEM((chunks * parts, max(8, second), LANES), f32),
            pltpu.VMEM((groups - 1, per, max(8, second), LANES), f32),
            pltpu.VMEM(latents.shape, f32),
            pltpu.VMEM((10, 8, channels), f32),
            pltpu.VMEM(small_shape, f32),
            pltpu.VMEM(small_shape, f32),
            pltpu.VMEM((groups,) + small_shape, f32),
            pltpu.VMEM((planes,) + small_shape, f32),
            dma((4,)), dma((2 + lines,)), dma((1 + lines, groups - 1)), dma((1 + lines, groups - 1)),
            dma((lines, groups - 1)), dma((lines, groups - 1)), dma((4,)), dma((4,)),
            dma((4,)), dma((4,)), to_sweep, to_sweep, to_z, to_z, dma((2, groups - 1)), dma((2, groups - 1)),
            one, one, to_sweep, to_sweep, to_z, to_z, one, dma((5,)),
            dma((4, planes - 1)), dma((4, planes - 1)), to_sweep, to_sweep,
        ],
        compiler_params=pltpu.CompilerParams(
            collective_id=0, has_side_effects=True, vmem_limit_bytes=BIG
        ),
        name="block",
    )(
        latents, cotangent.reshape(flat), conv_kernel, conv_bias.reshape(1, channels),
        norm_gain.reshape(1, channels), w_query, w_key, w_value, w_output,
    )
    half = pl.BlockSpec(
        (1, height // 2, width, channels), lambda i: (lax.div(i, 2), lax.rem(i, 2), 0, 0)
    )
    out_mat, line = sds((rows_each, inner), f32), sds((1, channels), f32)
    out = pl.pallas_call(
        functools.partial(finish_kernel, parts),
        out_shape=[
            sds(latents.shape, f32), sds(conv_kernel.shape, f32), line, line,
            out_mat, out_mat, out_mat, out_mat,
        ],
        grid=(sweeps * 2,),
        in_specs=[half, whole_block(fin.shape), whole_block(small_shape)],
        out_specs=[half] + [
            whole_block(shape)
            for shape in (conv_kernel.shape, line.shape, line.shape) + (out_mat.shape,) * 4
        ],
        compiler_params=pltpu.CompilerParams(vmem_limit_bytes=BIG),
        name="finish",
    )(raw_lat, fin, small)
    grad_latents, grad_kernel, grad_bias, grad_gain, *mats = out
    return (grad_latents, grad_kernel, grad_bias.reshape(channels), grad_gain.reshape(channels), *mats)


def solution(mesh):
    image = P("sweep", None, "azim", None)
    share = P("azim", None)
    return jax.shard_map(
        on_device,
        mesh=mesh,
        in_specs=(image, image) + (P(),) * 7,
        out_specs=(image, P(), P(), P(), share, share, share, share),
        check_vma=False,
    )
```

```python
import functools
import math

import jax
import jax.numpy as jnp
from jax import lax
from jax.experimental import pallas as pl
from jax.experimental.pallas import tpu as pltpu
from jax.sharding import PartitionSpec as P

DH = 64
EPS = 1e-06
LANES = 128
PIX = 16
MESH = pl.DeviceIdType.MESH
VMEM = pl.BlockSpec(memory_space=pltpu.VMEM)
ANY = pl.BlockSpec(memory_space=pl.ANY)
HBM = pl.BlockSpec(memory_space=pltpu.HBM)
MIB = 1024 * 1024
BIG = 56 * MIB


def remote(src, dst, send, recv, where):
    return pltpu.make_async_remote_copy(
        src_ref=src, dst_ref=dst, send_sem=send, recv_sem=recv, device_id=where, device_id_type=MESH
    )


def greet(partners):
    barrier = pltpu.get_barrier_semaphore()
    for where in partners:
        pl.semaphore_signal(barrier, inc=1, device_id=where, device_id_type=MESH)


def await_greetings(count):
    pl.semaphore_wait(pltpu.get_barrier_semaphore(), count)


def store_shifted(dst, s, h, val):
    width = val.shape[0]
    dst[1, s, h + 1] = val
    dst[0, s, h + 1] = pltpu.roll(val, 1, 0)
    dst[2, s, h + 1] = pltpu.roll(val, width - 1, 0)


def patch_edges(dst, left, right, sweeps, height, width):
    for s in range(sweeps):
        for h in range(height):
            i = s * height + h
            dst[0, s, h + 1, 0:1, :] = left[i : i + 1, :]
            dst[2, s, h + 1, width - 1 : width, :] = right[i : i + 1, :]


def zero_frame(dst, sweeps, height):
    for b in range(3):
        for s in range(sweeps):
            dst[b, s, 0] = jnp.zeros(dst.shape[3:], jnp.float32)
            dst[b, s, height + 1] = jnp.zeros(dst.shape[3:], jnp.float32)


def dot(a, b, dims):
    return lax.dot_general(a, b, (dims, ((), ())), preferred_element_type=jnp.float32)


NN = ((1,), (0,))
NT = ((1,), (1,))
TN = ((0,), (0,))


def block_kernel(
    groups, strips, heads, predivide,
    lat_hbm, cot_hbm, kern_hbm, bias_hbm, gain_hbm, wq_hbm, wk_hbm, wv_hbm, wo_hbm,
    out_lat, out_fin, out_small,
    lat, cot, kern, bias, gain_ref, act, gy, y_src, y_pix, cot_pix, grad, ret,
    fore_left, fore_right, fore_in_left, fore_in_right, edge_left, edge_right, in_left, in_right,
    weights, left_s, right_s, grad_att_s, mats, pair_buf, acc, sweep_buf, acc2, z_buf, early_z, early_sum, late_buf, lat_out,
    taps, small, small_pair, small_sweep, small_z,
    w_sem, own_sem, a2a_send, a2a_recv, back_send, back_recv, halo_send, halo_recv,
    pair_send, pair_recv, sweep_send, sweep_recv, z_send, z_recv, fin_send, fin_recv,
    sp_send, sp_recv, ss_send, ss_recv, sz_send, sz_recv, lat_sem, in_sem, ez_send, ez_recv, late_send, late_recv,
):
    sweeps, height, width, channels = lat.shape
    each = height * width // groups
    planes = strips // 2
    inner = right_s.shape[2]
    me = lax.axis_index("sweep")
    az = lax.axis_index("azim")
    core = lax.rem(az, 2)
    z = az // 2
    other = az + 1 - 2 * core
    right, left = lax.rem(az + 1, strips), lax.rem(az + strips - 1, strips)
    partners = [lax.rem(me + k, groups) for k in range(1, groups)]
    z_partners = [lax.rem(z + k, planes) for k in range(1, planes)]
    pending = []

    def send(*args):
        copy = remote(*args)
        copy.start()
        pending.append(copy)
        return copy

    greetings = (
        [{"sweep": g} for g in partners]
        + [{"azim": left}, {"azim": right}, {"azim": other}]
        + [{"azim": p * 2 + core} for p in z_partners]
    )
    greet(greetings)
    inputs = []
    for i, (source, target) in enumerate(
        ((lat_hbm, lat), (cot_hbm, cot), (kern_hbm, kern), (bias_hbm, bias), (gain_hbm, gain_ref))
    ):
        inputs.append(pltpu.make_async_copy(source, target, in_sem.at[i]))
        inputs[-1].start()
    loads = []
    for i, w in enumerate((wq_hbm, wk_hbm, wv_hbm, wo_hbm)):
        loads.append(pltpu.make_async_copy(w, weights.at[i], w_sem.at[i]))
        loads[-1].start()
    mine = pl.ds(pl.multiple_of(me * each, PIX), each)
    slots = pl.ds(me * sweeps, sweeps)

    inputs[0].wait()
    for s in range(sweeps):
        for h in range(height):
            i = s * height + h
            fore_left[i : i + 1, :] = lat[s, h, 0:16, :].astype(jnp.float32)[0:1]
            fore_right[i : i + 1, :] = lat[s, h, width - 16 : width, :].astype(jnp.float32)[15:16]
    await_greetings(len(greetings))
    to_right = send(fore_right, fore_in_left, halo_send.at[0], halo_recv.at[0], {"azim": right})
    to_left = send(fore_left, fore_in_right, halo_send.at[1], halo_recv.at[1], {"azim": left})

    def give(k, g, source, target, stage, count, send_sem, recv_sem):
        there = pl.ds(pl.multiple_of(g * each + stage * count, PIX), count)
        here = slice(stage * count, (stage + 1) * count)
        return send(source.at[:, there, :], target.at[slots, here, :], send_sem, recv_sem, {"sweep": g})

    inputs[1].wait()
    cot_copies = [give(k, g, cot, cot_pix, 0, each, a2a_send.at[0, k], a2a_recv.at[0, k]) for k, g in enumerate(partners)]
    cot_own = pltpu.make_async_copy(cot.at[:, mine, :], cot_pix.at[slots], own_sem.at[0])
    cot_own.start()

    for copy in inputs[2:]:
        copy.wait()
    for s in range(sweeps):
        def activate(h, carry, s=s):
            x = lat[s, h].astype(jnp.float32)
            store_shifted(act, s, h, x / (1.0 + jnp.exp(-x)))
            return carry
        lax.fori_loop(0, height, activate, 0)
    zero_frame(act, sweeps, height)
    zero_frame(gy, sweeps, height)
    taps[...] = jnp.zeros(taps.shape, jnp.float32)
    to_right.wait_recv()
    to_left.wait_recv()
    for ref in (fore_in_left, fore_in_right):
        x = ref[...]
        ref[...] = x / (1.0 + jnp.exp(-x))
    patch_edges(act, fore_in_left, fore_in_right, sweeps, height, width)

    def convolve_row(s, h):
        total = lat[s, h].astype(jnp.float32) + bias[...]
        for a in range(3):
            for b in range(3):
                total = total + kern[3 * a + b : 3 * a + b + 1, :] * act[b, s, h + a]
        y_src[s, pl.ds(pl.multiple_of(h * width, PIX), width), :] = total.astype(jnp.bfloat16)

    lines = height // groups if groups <= height else 1
    count = each // lines
    y_copies = [[] for _ in range(lines)]

    def give_y(k, g, stage):
        y_copies[stage].append(
            give(k, g, y_src, y_pix, stage, count, a2a_send.at[1 + stage, k], a2a_recv.at[1 + stage, k])
        )

    if groups <= height:
        for stage in range(lines):
            for k, g in enumerate(partners + [me]):
                for sweep in range(sweeps):
                    convolve_row(sweep, g * lines + stage)
                if k < groups - 1:
                    give_y(k, g, stage)
    else:
        def whole(i, carry):
            convolve_row(i // height, i % height)
            return carry
        lax.fori_loop(0, sweeps * height, whole, 0)
        for k, g in enumerate(partners):
            give_y(k, g, 0)
    y_own = pltpu.make_async_copy(y_src.at[:, mine, :], y_pix.at[slots], own_sem.at[1])
    y_own.start()

    m = groups * sweeps * PIX
    blocks = each // PIX
    total_sweeps = groups * sweeps
    scale = 1.0 / math.sqrt(DH)
    gain = gain_ref[...]
    for load in loads:
        load.wait()
    for copy in cot_copies:
        copy.wait_recv()
    cot_own.wait()
    for block in range(blocks):
        at = slice(block * PIX, (block + 1) * PIX)
        own = slice(block * m, (block + 1) * m)
        rows = cot_pix[:, at, :].reshape(m, channels)
        left_s[1, own, :] = rows
        grad_att_s[own, :] = dot(rows, weights[3], NN).astype(jnp.bfloat16)
    row_pix = lax.broadcasted_iota(jnp.int32, (m, m), 0) % PIX
    col_pix = lax.broadcasted_iota(jnp.int32, (m, m), 1) % PIX
    same = row_pix == col_pix
    same = jnp.concatenate([same] * heads, axis=0)
    lane_head = lax.broadcasted_iota(jnp.int32, (1, inner), 1) // DH

    def spread(value):
        return jnp.concatenate(
            [jnp.where(lane_head == h, value, jnp.zeros_like(value)) for h in range(heads)], axis=0
        )

    def collect(value):
        total = jnp.where(lane_head == 0, value[0:m], 0.0)
        for h in range(1, heads):
            total = jnp.where(lane_head == h, value[h * m : (h + 1) * m], total)
        return total

    y_own.wait()
    back, back_own = [], []
    gain_total = jnp.zeros((1, channels), jnp.float32)
    several = count // PIX
    for stage in range(lines):
        for copy in y_copies[stage]:
            copy.wait_recv()
        base = stage * count
        span = slice(stage * several * m, (stage + 1) * several * m)
        y = jnp.concatenate(
            [
                y_pix[:, base + i * PIX : base + (i + 1) * PIX, :].reshape(m, channels)
                for i in range(several)
            ],
            axis=0,
        ).astype(jnp.float32)
        root = jnp.sqrt(jnp.mean(y * y, axis=-1, keepdims=True) + EPS)
        inverse = 1.0 / root
        normed = (y * inverse * gain).astype(jnp.bfloat16)
        left_s[0, span, :] = normed
        queries = dot(normed, weights[0], NN).astype(jnp.bfloat16)
        keys = dot(normed, weights[1], NN).astype(jnp.bfloat16)
        values = dot(normed, weights[2], NN).astype(jnp.bfloat16)
        grads = []
        for i in range(several):
            part = slice(i * m, (i + 1) * m)
            own = slice((stage * several + i) * m, (stage * several + i + 1) * m)
            key, value = keys[part], values[part]
            query_x = spread(queries[part])
            grad_att_x = spread(grad_att_s[own, :])
            scores = jnp.where(same, dot(query_x, key, NT) * scale, -1e30)
            top = jnp.max(scores, axis=-1, keepdims=True)
            expon = jnp.exp(scores - top)
            probs = expon / jnp.sum(expon, axis=-1, keepdims=True)
            probs_low = probs.astype(jnp.bfloat16)
            right_s[3, own, :] = collect(dot(probs_low, value, NN)).astype(jnp.bfloat16)
            grad_probs = dot(grad_att_x, value, NT)
            inner_sum = jnp.sum(probs * grad_probs, axis=-1, keepdims=True)
            grad_scores = (probs * (grad_probs - inner_sum) * scale).astype(jnp.bfloat16)
            grad_v = dot(probs_low, grad_att_x, TN).astype(jnp.bfloat16)
            grad_q = collect(dot(grad_scores, key, NN)).astype(jnp.bfloat16)
            grad_k = dot(grad_scores, query_x, TN).astype(jnp.bfloat16)
            right_s[0, own, :] = grad_q
            right_s[1, own, :] = grad_k
            right_s[2, own, :] = grad_v
            grads.append((grad_q, grad_k, grad_v))
        grad_q, grad_k, grad_v = (jnp.concatenate(each_grad, axis=0) for each_grad in zip(*grads))
        grad_normed = (
            dot(grad_q, weights[0], NT) + dot(grad_k, weights[1], NT) + dot(grad_v, weights[2], NT)
        )
        gain_total = gain_total + jnp.sum(grad_normed * y * inverse, axis=0, keepdims=True)
        gained = grad_normed * gain
        mean = jnp.mean(gained * y, axis=-1, keepdims=True)
        grad_attn = (inverse * (gained - y * mean * inverse * inverse)).astype(jnp.bfloat16)
        for i in range(several):
            at = slice(base + i * PIX, base + (i + 1) * PIX)
            grad[:, at, :] = grad_attn[i * m : (i + 1) * m].reshape(total_sweeps, PIX, channels)
        at = slice(base, base + count)
        here = pl.ds(pl.multiple_of(me * each + base, PIX), count)
        for k, g in enumerate(partners):
            back.append(
                send(
                    grad.at[pl.ds(g * sweeps, sweeps), at, :], ret.at[:, here, :],
                    back_send.at[stage, k], back_recv.at[stage, k], {"sweep": g},
                )
            )
        back_own.append(
            pltpu.make_async_copy(grad.at[slots, at, :], ret.at[:, here, :], own_sem.at[2 + stage])
        )
        back_own[-1].start()

    _, lanes, _, _, parts, rows, _ = mats.shape
    per = 4 * lanes * parts // groups
    interleave = groups == 4
    order = [lax.rem(me + k + 1, 4) if interleave else k for k in range(4)]
    scatter, early = [], []
    units = lanes * parts
    split = rows - rows * 3 // 8 // 8 * 8

    def scatter_to(k, g):
        scatter.append(
            send(acc.at[pl.ds(g * per, per), :, 0:split], sweep_buf.at[k], sweep_send.at[k], sweep_recv.at[k], {"sweep": g})
        )

    pairs = []

    def form(n):
        i = order[n]
        full = dot(left_s[i // 3], right_s[i], TN)
        for j in range(lanes):
            part = full[:, j * LANES : (j + 1) * LANES]
            mats[i, j] = part.reshape(planes, 2, parts, rows, LANES)
        pairs.append(
            send(mats.at[i, :, :, 1 - core], pair_buf.at[i], pair_send.at[n], pair_recv.at[n], {"azim": other})
        )

    form(0)
    form(1)
    for n, i in enumerate(order):
        if n + 2 < 4:
            form(n + 2)
        pairs[n].wait_recv()
        for j in range(lanes):
            for p in range(parts):
                for q in range(planes):
                    acc[(i * lanes + j) * parts + p, q] = mats[i, j, q, core, p] + pair_buf[i, j, q, p]
        if interleave and n < 3:
            scatter_to(n, i)
        if split < rows:
            of = pl.ds(i * units, units)
            for k, p in enumerate(z_partners):
                early.append(
                    send(
                        acc.at[of, p, split:rows], early_z.at[k, of], ez_send.at[n, k], ez_recv.at[n, k],
                        {"azim": p * 2 + core},
                    )
                )
    if not interleave:
        for k, g in enumerate(partners):
            scatter_to(k, g)

    for copy in back:
        copy.wait_recv()
    for copy in back_own:
        copy.wait()
    for s in range(sweeps):
        def combine(h, carry, s=s):
            at = pl.ds(pl.multiple_of(h * width, PIX), width)
            val = cot[s, at, :].astype(jnp.float32) + ret[s, at, :].astype(jnp.float32)
            store_shifted(gy, s, h, val)
            edge_left[pl.ds(s * height + h, 1), :] = val[0:1]
            edge_right[pl.ds(s * height + h, 1), :] = val[width - 1 : width]
            return carry
        lax.fori_loop(0, height, combine, 0)
    to_right = send(edge_right, in_left, halo_send.at[2], halo_recv.at[2], {"azim": right})
    to_left = send(edge_left, in_right, halo_send.at[3], halo_recv.at[3], {"azim": left})

    def fold(v):
        return sum(v[8 * i : 8 * i + 8] for i in range(1, width // 8)) + v[0:8]

    for s in range(sweeps):
        def weigh(h, carry, s=s):
            mid = gy[1, s, h + 1]
            for t in range(9):
                taps[t] = taps[t] + fold(mid * act[t % 3, s, h + t // 3])
            taps[9] = taps[9] + fold(mid)
            return carry
        lax.fori_loop(0, height, weigh, 0)
    small[...] = jnp.zeros(small.shape, jnp.float32)
    for t in range(10):
        small[t : t + 1, :] = jnp.sum(taps[t], axis=0, keepdims=True) * predivide
    small[10:11, :] = gain_total * predivide
    sp = send(small, small_pair, sp_send, sp_recv, {"azim": other})

    late = []
    if split < rows:
        for copy in early:
            copy.wait_recv()
        for k, g in enumerate(partners + [me]):
            for i in range(per):
                u = g * per + i
                total = acc[u, z, split:rows]
                for j in range(planes - 1):
                    total = total + early_z[j, u]
                early_sum[u] = total
            if k < groups - 1:
                late.append(
                    send(
                        early_sum.at[pl.ds(g * per, per)], late_buf.at[k], late_send.at[k], late_recv.at[k],
                        {"sweep": g},
                    )
                )
    for copy in scatter:
        copy.wait_recv()
    along = []
    for k, p in enumerate(z_partners + [z]):
        for i in range(per):
            total = acc[me * per + i, p, 0:split]
            for j in range(groups - 1):
                total = total + sweep_buf[j, i, p]
            acc2[p, i] = total
        if k < planes - 1:
            along.append(
                send(acc2.at[p], z_buf.at[k], z_send.at[k], z_recv.at[k], {"azim": p * 2 + core})
            )

    sp.wait_recv()
    small_sweep[me] = small[...] + small_pair[...]
    ss = []
    for k, g in enumerate(partners):
        ss.append(
            send(small_sweep.at[me], small_sweep.at[me], ss_send.at[k], ss_recv.at[k], {"sweep": g})
        )

    to_right.wait_recv()
    to_left.wait_recv()
    patch_edges(gy, in_left, in_right, sweeps, height, width)
    for s in range(sweeps):
        def convolve(h, carry, s=s):
            mid = gy[1, s, h + 1]
            total = jnp.zeros(mid.shape, jnp.float32)
            for a in range(3):
                for b in range(3):
                    t = 3 * a + b
                    total = total + kern[t : t + 1, :] * gy[2 - b, s, h + 2 - a]
            x = lat[s, h].astype(jnp.float32)
            sig = 1.0 / (1.0 + jnp.exp(-x))
            lat_out[s, h] = mid + total * (sig * (1.0 + x * (1.0 - sig)))
            return carry
        lax.fori_loop(0, height, convolve, 0)
    lat_copy = pltpu.make_async_copy(lat_out, out_lat, lat_sem)
    lat_copy.start()

    for copy in ss:
        copy.wait_recv()
    total = small_sweep[0]
    for g in range(1, groups):
        total = total + small_sweep[g]
    small_z[z] = total
    sz = []
    for k, p in enumerate(z_partners):
        sz.append(
            send(small_z.at[z], small_z.at[z], sz_send.at[k], sz_recv.at[k], {"azim": p * 2 + core})
        )

    gather = []
    if split < rows:
        for copy in late:
            copy.wait_recv()
        for i in range(per):
            total = early_sum[me * per + i]
            for k in range(groups - 1):
                total = total + late_buf[k, i]
            out_fin[me, i, split:rows] = total * predivide
        for k, g in enumerate(partners):
            some = out_fin.at[me, :, split:rows]
            gather.append(send(some, some, fin_send.at[1, k], fin_recv.at[1, k], {"sweep": g}))
    for copy in along:
        copy.wait_recv()
    for i in range(per):
        total = acc2[z, i]
        for k in range(planes - 1):
            total = total + z_buf[k, i]
        out_fin[me, i, 0:split] = total * predivide
    for k, g in enumerate(partners):
        some = out_fin.at[me, :, 0:split]
        gather.append(send(some, some, fin_send.at[0, k], fin_recv.at[0, k], {"sweep": g}))
    for copy in sz:
        copy.wait_recv()
    total = small_z[0]
    for p in range(1, planes):
        total = total + small_z[p]
    out_small[...] = total
    for copy in gather:
        copy.wait_recv()
    for copy in pending:
        copy.wait_send()
    lat_copy.wait()


def finish_kernel(parts, lat, fin, small, out_lat, out_kern, out_bias, out_gain, out_q, out_k, out_v, out_o):
    out_lat[...] = lat[...]

    @pl.when(pl.program_id(0) == 0)
    def unpack():
        groups, per, rows, _ = fin.shape
        lanes = groups * per // parts // 4
        for g in range(groups):
            for i in range(per):
                c, p = divmod(g * per + i, parts)
                out = (out_q, out_k, out_v, out_o)[c // lanes]
                j = c % lanes
                out[p * rows : (p + 1) * rows, j * LANES : (j + 1) * LANES] = fin[g, i]
        out_kern[...] = small[0:9, :]
        out_bias[...] = small[9:10, :]
        out_gain[...] = small[10:11, :]


def whole_block(shape):
    return pl.BlockSpec(shape, lambda i: (0,) * len(shape))


def on_device(
    latents, cotangent, conv_kernel, conv_bias, norm_gain, w_query, w_key, w_value, w_output
):
    f32, bf16 = jnp.float32, jnp.bfloat16
    dma = pltpu.SemaphoreType.DMA
    sds = jax.ShapeDtypeStruct
    sweeps, height, width, channels = latents.shape
    inner = w_query.shape[1]
    groups = lax.axis_size("sweep")
    strips = lax.axis_size("azim")
    planes = strips // 2
    each = height * width // groups
    total = sweeps * groups
    tokens = total * each
    edge = pltpu.VMEM((sweeps * height, channels), f32)
    framed = pltpu.VMEM((3, sweeps, height + 2, width, channels), f32)
    flat = (sweeps, height * width, channels)
    pixels = pltpu.VMEM((total, each, channels), bf16)
    lanes = inner // LANES
    chunks = 4 * lanes
    rows_each = channels // strips
    parts = max(1, groups // chunks)
    rows = rows_each // parts
    per = chunks * parts // groups
    predivide = 1.0 / math.sqrt(total * height * width * strips)
    small_shape = (16, channels)
    lines = height // groups if groups <= height else 1
    second = rows * 3 // 8 // 8 * 8
    to_sweep, to_z, one = dma((groups - 1,)), dma((planes - 1,)), dma(())

    raw_lat, fin, small = pl.pallas_call(
        functools.partial(block_kernel, groups, strips, inner // DH, predivide),
        out_shape=[
            sds(latents.shape, f32), sds((groups, per, rows, LANES), f32), sds(small_shape, f32),
        ],
        in_specs=[HBM] * 9,
        out_specs=[ANY, VMEM, VMEM],
        scratch_shapes=[
            pltpu.VMEM(latents.shape, bf16), pltpu.VMEM(flat, bf16), pltpu.VMEM(conv_kernel.shape, f32),
            pltpu.VMEM((1, channels), f32), pltpu.VMEM((1, channels), f32),
            framed, framed, pltpu.VMEM(flat, bf16), pixels, pixels, pixels, pltpu.VMEM(flat, bf16),
            edge, edge, edge, edge, edge, edge, edge, edge,
            pltpu.VMEM((4, channels, inner), bf16),
            pltpu.VMEM((2, tokens, channels), bf16),
            pltpu.VMEM((4, tokens, inner), bf16),
            pltpu.VMEM((tokens, inner), bf16),
            pltpu.VMEM((4, lanes, planes, 2, parts, rows, LANES), f32),
            pltpu.VMEM((4, lanes, planes, parts, rows, LANES), f32),
            pltpu.VMEM((chunks * parts, planes, rows, LANES), f32),
            pltpu.VMEM((groups - 1, per, planes, rows - second, LANES), f32),
            pltpu.VMEM((planes, per, rows - second, LANES), f32),
            pltpu.VMEM((planes - 1, per, rows - second, LANES), f32),
            pltpu.VMEM((planes - 1, chunks * parts, max(8, second), LANES), f32),
            pltpu.VMEM((chunks * parts, max(8, second), LANES), f32),
            pltpu.VMEM((groups - 1, per, max(8, second), LANES), f32),
            pltpu.VMEM(latents.shape, f32),
            pltpu.VMEM((10, 8, channels), f32),
            pltpu.VMEM(small_shape, f32),
            pltpu.VMEM(small_shape, f32),
            pltpu.VMEM((groups,) + small_shape, f32),
            pltpu.VMEM((planes,) + small_shape, f32),
            dma((4,)), dma((2 + lines,)), dma((1 + lines, groups - 1)), dma((1 + lines, groups - 1)),
            dma((lines, groups - 1)), dma((lines, groups - 1)), dma((4,)), dma((4,)),
            dma((4,)), dma((4,)), to_sweep, to_sweep, to_z, to_z, dma((2, groups - 1)), dma((2, groups - 1)),
            one, one, to_sweep, to_sweep, to_z, to_z, one, dma((5,)),
            dma((4, planes - 1)), dma((4, planes - 1)), to_sweep, to_sweep,
        ],
        compiler_params=pltpu.CompilerParams(
            collective_id=0, has_side_effects=True, vmem_limit_bytes=BIG if total > 8 else 32 * MIB
        ),
        name="block",
    )(
        latents, cotangent.reshape(flat), conv_kernel, conv_bias.reshape(1, channels),
        norm_gain.reshape(1, channels), w_query, w_key, w_value, w_output,
    )
    half = pl.BlockSpec(
        (1, height, width, channels), lambda i: (i, 0, 0, 0)
    )
    out_mat, line = sds((rows_each, inner), f32), sds((1, channels), f32)
    out = pl.pallas_call(
        functools.partial(finish_kernel, parts),
        out_shape=[
            sds(latents.shape, f32), sds(conv_kernel.shape, f32), line, line,
            out_mat, out_mat, out_mat, out_mat,
        ],
        grid=(sweeps,),
        in_specs=[half, whole_block(fin.shape), whole_block(small_shape)],
        out_specs=[half] + [
            whole_block(shape)
            for shape in (conv_kernel.shape, line.shape, line.shape) + (out_mat.shape,) * 4
        ],
        compiler_params=pltpu.CompilerParams(vmem_limit_bytes=16 * MIB),
        name="finish",
    )(raw_lat, fin, small)
    grad_latents, grad_kernel, grad_bias, grad_gain, *mats = out
    return (grad_latents, grad_kernel, grad_bias.reshape(channels), grad_gain.reshape(channels), *mats)


def solution(mesh):
    image = P("sweep", None, "azim", None)
    share = P("azim", None)
    return jax.shard_map(
        on_device,
        mesh=mesh,
        in_specs=(image, image) + (P(),) * 7,
        out_specs=(image, P(), P(), P(), share, share, share, share),
        check_vma=False,
    )
```
